256 devices in a mesh: cell: 32 (over x, y, core), mem: 8 (over z).
Axes of the slice: x: 4, y: 4, z: 8, core: 2. Of those that a mesh axis runs over, the one named last changes fastest.
Arguments:
- ensemble: float32 [256, 65536], P('mem', 'cell'), may hold values from -6 to 6
- weights: float32 [4, 128, 512], replicated, may hold values from -0.25 to 0.25
- blocks: int32 [4, 128, 8], replicated, may hold values from 0 to 1023
- owner_ids: int32 [4], replicated, may hold values from 0 to 31
- counts: int32 [4], replicated, may hold values from 64 to 128, as said below
- obs_values: float32 [128, 128], P('cell'), may hold values from -8 to 8
- obs_error: float32 [128, 128], P('cell'), may hold values from 0.3 to 3
Outputs:
- posterior: float32 [256, 65536], P('mem', 'cell')
The draws below stay inside these ranges and needn't reach their ends.
Inputs may be any that keep to these rules, and one draw needn't show every extreme that they name: Observations o < counts[b] of batch b are live; one batch has all 128 live, another 128 // 2.
All inputs are finite; a program needn't handle non-finite values.
Results may differ from the reference program's by a relative error of at most 0.00015.
Values sent between devices are 32-bit elements; how exact they have to be, the bound alone decides.
No kernel may reach another device: no remote copies, remote signals or barrier semaphores. Data moves between devices by JAX's collectives and lax.ppermute only.
A program may use at most 64 MiB of HBM per device.

```python
import math
import jax
import jax.numpy as jnp
from jax import lax

MEMBERS = 256
NOBS = 128
NB = 4
FB = 8
BLK = 64
CELLS = 65536
NBLOCKS = 1024
N_CELL = 32


def draw_counts(key, part):
    key = jax.random.fold_in(key, 7)
    first_key, second_key = jax.random.split(key)
    drawn = jax.random.randint(first_key, (NB,), NOBS // 2, NOBS + 1)
    chosen = jax.random.randint(second_key, (), 0, NB)
    slots = jnp.arange(NB, dtype=jnp.int32)
    drawn = jnp.where(slots == chosen, NOBS, drawn)
    drawn = jnp.where(slots == (chosen + 1) % NB, NOBS // 2, drawn)
    return drawn.astype(jnp.int32)


def with_ends(result, own_key, smallest, largest):
    longest = result.shape.index(max(result.shape))
    spots = []
    for shift in (0, 1):
        where = [jax.random.randint(jax.random.fold_in(own_key, axis), (), 0, length) for axis, length in enumerate(result.shape)]
        where[longest] = (where[longest] + shift) % result.shape[longest]
        spots.append(tuple(where))
    return result.at[spots[0]].set(smallest).at[spots[1]].set(largest)


def steps_of(stream_key, extent, cuts, least, top_value):
    gain = 1.0
    for dim, shards_of in cuts:
        steps = jax.random.uniform(jax.random.fold_in(jax.random.fold_in(stream_key, 6), dim), (shards_of,), jnp.float32, least / len(cuts), top_value / len(cuts))
        gain = gain * jnp.repeat(jnp.exp(steps), extent[dim] // shards_of).reshape((-1,) + (1,) * (len(extent) - 1 - dim))
    return gain


def normal_values(own_key, shape, width, reach, cuts=(), kind=jnp.bfloat16):
    array = width * jax.random.normal(own_key, shape, jnp.float32)
    if cuts:
        array = array * steps_of(own_key, shape, cuts, -0.22, 0.18)
    return jnp.clip(array, -reach, reach).astype(kind)


def setup_inputs(seed: int = 0) -> dict:
    seeds = jax.random.split(jax.random.key(seed), 8)
    ensemble = normal_values(seeds[0], (MEMBERS, CELLS), 1.0, 6.0, ((0, 8), (1, 32)), jnp.float32)
    weights = normal_values(seeds[1], (NB, NOBS, FB * BLK), (FB * BLK) ** -0.5, 0.25, (), jnp.float32)
    blocks = with_ends(jax.random.randint(seeds[2], (NB, NOBS, FB), 0, NBLOCKS), jax.random.fold_in(seeds[2], 1), 0, NBLOCKS - 1).astype(jnp.int32)
    owner_ids = with_ends(jax.random.randint(seeds[3], (NB,), 0, N_CELL), jax.random.fold_in(seeds[3], 1), 0, N_CELL - 1).astype(jnp.int32)
    counts = draw_counts(jax.random.fold_in(seeds[7], 71), 0)
    obs_values = normal_values(seeds[5], (N_CELL * NB, NOBS), 1.5, 8.0, ((0, 32),), jnp.float32)
    obs_error = jnp.clip(jnp.exp(math.log(3.0) - 2.3025851 * jax.random.uniform(seeds[6], (N_CELL * NB, NOBS), jnp.float32) ** steps_of(seeds[6], (N_CELL * NB, NOBS), ((0, 32),), -0.2, 0.2)), 0.3, 3.0)
    return dict(ensemble=ensemble, weights=weights, blocks=blocks, owner_ids=owner_ids, counts=counts, obs_values=obs_values, obs_error=obs_error)


HIGH = lax.Precision.HIGHEST

def analysis(gathered, values, spread, count):
    members = gathered.shape[1]
    valid_rows = jnp.arange(NOBS, dtype=jnp.int32) < count
    prior_mean = jnp.sum(gathered, 1) / members
    obs_pert = (gathered - prior_mean[:, None]) * valid_rows.astype(jnp.float32)[:, None]
    innovation = jnp.where(valid_rows, values - prior_mean, jnp.float32(0.0))
    noise_sd = jnp.where(valid_rows, spread, jnp.float32(1.0))
    innov_cov = jnp.dot(obs_pert, obs_pert.T, precision=HIGH) / (members - 1) + jnp.diag(noise_sd * noise_sd)
    factor = jnp.linalg.cholesky(innov_cov)
    mixed_rows = lax.linalg.triangular_solve(factor + jnp.diag(noise_sd), obs_pert, left_side=True, lower=True)
    transform = lax.linalg.triangular_solve(factor, mixed_rows, left_side=True, lower=True, transpose_a=True)
    half_solved = lax.linalg.triangular_solve(factor, innovation[:, None], left_side=True, lower=True)
    solved = lax.linalg.triangular_solve(factor, half_solved, left_side=True, lower=True, transpose_a=True)[:, 0]
    return (obs_pert, solved, transform)

def reference(ensemble, weights, blocks, owner_ids, counts, obs_values, obs_error):
    average = jnp.mean(ensemble, 0)
    perturbation = ensemble - average[None, :]
    factor_k = MEMBERS - 1
    offsets = jnp.arange(BLK, dtype=jnp.int32)
    for batch_no in range(NB):
        state_now = average[None, :] + perturbation
        columns = blocks[batch_no][:, :, None] * BLK + offsets[None, None, :]
        picked = state_now[:, columns]
        batch_weights = weights[batch_no].reshape(NOBS, FB, BLK)
        priors = jnp.einsum('mofj,ofj->om', picked, batch_weights, precision=HIGH)
        row_no = owner_ids[batch_no] * NB + batch_no
        obs_pert, solved, transform = analysis(priors, obs_values[row_no], obs_error[row_no], counts[batch_no])
        crossed = jnp.dot(obs_pert, perturbation, precision=HIGH)
        average = average + jnp.dot(solved, crossed, precision=HIGH) / factor_k
        perturbation = perturbation - jnp.dot(transform.T, crossed, precision=HIGH) / factor_k
    return average[None, :] + perturbation
```

```python
import jax
import jax.numpy as jnp
from jax import lax
from jax.experimental import pallas as pl
from jax.experimental.pallas import tpu as pltpu
from jax.sharding import PartitionSpec as P

MEMBERS = 256
NOBS = 128
NB = 4
FB = 8
BLK = 64
LANES = 128
SUB = 8
HIGH = lax.Precision.HIGHEST
VMEM = pl.BlockSpec(memory_space=pltpu.VMEM)
SMEM = pl.BlockSpec(memory_space=pltpu.SMEM)
ANY = pl.BlockSpec(memory_space=pl.ANY)


def dot(a, b, ca=1, cb=0):
    return lax.dot_general(a, b, (((ca,), (cb,)), ((), ())), precision=HIGH)


def priors_kernel(place_ref, state_ref, weights_ref, blocks_ref, values_ref, error_ref, out_ref, operator):
    batch = pl.program_id(0)
    members, cells = state_ref.shape
    first = place_ref[0] * (cells // BLK)
    half = lax.broadcasted_iota(jnp.int32, (SUB, LANES), 1) // BLK

    def rows(tile, carry):
        at = pl.multiple_of(tile * SUB, SUB)
        block = blocks_ref[0, pl.ds(at, SUB), :] - first
        entries = weights_ref[0, pl.ds(at, SUB), :]
        groups, parts = [], []
        for f in range(FB):
            pair = entries[:, (f // 2) * LANES : (f // 2 + 1) * LANES]
            swapped = pltpu.roll(pair, BLK, 1)
            both = jnp.where(half == f % 2, pair, swapped)
            index = jnp.broadcast_to(block[:, f : f + 1], (SUB, LANES))
            parts.append(jnp.where(index % 2 == half, both, 0.0))
            groups.append(jnp.where(index < 0, -1, index // 2))
        for g in range(cells // LANES):
            total = jnp.where(groups[0] == g, parts[0], 0.0)
            for f in range(1, FB):
                total = total + jnp.where(groups[f] == g, parts[f], 0.0)
            operator[pl.ds(at, SUB), g * LANES : (g + 1) * LANES] = total
        return carry

    lax.fori_loop(0, NOBS // SUB, rows, 0)
    out_ref[:members, :] = dot(state_ref[...], operator[...], 1, 1)
    mine = (place_ref[1 + batch] == place_ref[0]).astype(jnp.float32)
    out_ref[members : members + 1, :] = values_ref[pl.ds(batch, 1), :] * mine
    out_ref[members + 1 : members + 2, :] = error_ref[pl.ds(batch, 1), :] * mine
    out_ref[members + 2 :, :] = jnp.zeros((SUB - 2, LANES), jnp.float32)


def local_priors(place, state, weights, blocks, values, error):
    members, cells = state.shape
    return pl.pallas_call(
        priors_kernel,
        grid=(NB,),
        out_shape=jax.ShapeDtypeStruct((members + SUB, NB * NOBS), jnp.float32),
        in_specs=[
            SMEM,
            pl.BlockSpec((members, cells), lambda b: (0, 0)),
            pl.BlockSpec((1, NOBS, FB * BLK), lambda b: (b, 0, 0)),
            pl.BlockSpec((1, NOBS, FB), lambda b: (b, 0, 0)),
            pl.BlockSpec((NB, NOBS), lambda b: (0, 0)),
            pl.BlockSpec((NB, NOBS), lambda b: (0, 0)),
        ],
        out_specs=pl.BlockSpec((members + SUB, NOBS), lambda b: (0, b)),
        scratch_shapes=[pltpu.VMEM((NOBS, cells), jnp.float32)],
        compiler_params=pltpu.CompilerParams(vmem_limit_bytes=32 << 20),
        name="priors",
    )(place, state, weights, blocks, values, error)


def eliminate(cov, noise):
    tiles = NOBS // SUB
    sub = lax.broadcasted_iota(jnp.int32, (SUB, LANES), 0)
    lane = lax.broadcasted_iota(jnp.int32, (SUB, LANES), 1)
    noise_cols = jnp.broadcast_to(noise, (NOBS, LANES)).T
    r = [cov[i * SUB : (i + 1) * SUB, :] for i in range(tiles)]
    z = [jnp.where(lane == sub + i * SUB, 1.0, 0.0) for i in range(tiles)]
    y = list(z)
    for j in range(NOBS):
        t, s = j // SUB, j % SUB
        col = {i: jnp.broadcast_to(r[i][:, j : j + 1], (SUB, LANES)) for i in range(t, tiles)}
        pivot = jnp.broadcast_to(col[t][s : s + 1, :], (SUB, LANES))
        inv = 1.0 / pivot
        root = lax.rsqrt(pivot)
        shifted = 1.0 / (pivot * root + jnp.broadcast_to(noise_cols[j : j + 1, :], (SUB, LANES)))
        row_r = jnp.broadcast_to(r[t][s : s + 1, :], (SUB, LANES)) * inv
        row_z = jnp.broadcast_to(z[t][s : s + 1, :], (SUB, LANES)) * inv
        row_y = jnp.broadcast_to(y[t][s : s + 1, :], (SUB, LANES)) * (root * shifted)
        z[t] = jnp.where(sub == s, z[t] * root, z[t])
        y[t] = jnp.where(sub == s, y[t] * shifted, y[t])
        if s < SUB - 1:
            col[t] = jnp.where(sub > s, col[t], 0.0)
        else:
            del col[t]
        for i in col:
            r[i] = r[i] - col[i] * row_r
            z[i] = z[i] - col[i] * row_z
            y[i] = y[i] - col[i] * row_y
    return jnp.concatenate(z, 0), jnp.concatenate(y, 0)


def analysis_kernel(counts_ref, obs_ref, *refs):
    members = MEMBERS // 8
    parts, out_ref, state = refs[:8], refs[8], refs[9]
    for k in range(8):
        state[k * members : (k + 1) * members, : NB * NOBS] = parts[k][...]
    wide = NB * NOBS + MEMBERS
    eye = lax.broadcasted_iota(jnp.int32, (MEMBERS, MEMBERS), 0) == lax.broadcasted_iota(
        jnp.int32, (MEMBERS, MEMBERS), 1
    )
    state[:, NB * NOBS :] = jnp.where(eye, 1.0, 0.0)
    lanes = lax.broadcasted_iota(jnp.int32, (1, LANES), 1)
    diagonal = lax.broadcasted_iota(jnp.int32, (NOBS, LANES), 0) == lax.broadcasted_iota(
        jnp.int32, (NOBS, LANES), 1
    )
    scale = 1.0 / (MEMBERS - 1)
    for b in range(NB):
        here = slice(b * NOBS, (b + 1) * NOBS)
        live = lanes < counts_ref[b]
        priors = state[:, here]
        mean = jnp.sum(priors, 0, keepdims=True) * (1.0 / MEMBERS)
        pert = jnp.where(live, priors - mean, 0.0)
        innovation = jnp.where(live, obs_ref[0:1, here] - mean, 0.0)
        noise = jnp.where(live, obs_ref[1:2, here], 1.0)
        pert_t = pert.T
        cov = dot(pert_t, pert) * scale + jnp.where(diagonal, noise * noise, 0.0)
        crossed = dot(pert_t, state[:, (b + 1) * NOBS :])
        inv_l, inv_ld = eliminate(cov, noise)
        half = dot(inv_l, crossed)
        solved = dot(innovation, inv_l, 1, 1)
        if b < NB - 1:
            gain = (solved - dot(pert, inv_ld, 1, 1)) * scale
            state[:, (b + 1) * NOBS :] = state[:, (b + 1) * NOBS :] + dot(gain, half)
        else:
            gain = (solved - dot(pert[:members], inv_ld, 1, 1)) * scale
            out_ref[...] = state[:members, NB * NOBS : wide] + dot(gain, half)


def analysis(counts, obs, parts):
    members = MEMBERS // 8
    return pl.pallas_call(
        analysis_kernel,
        out_shape=jax.ShapeDtypeStruct((members, MEMBERS), jnp.float32),
        in_specs=[SMEM, VMEM] + [VMEM] * 8,
        out_specs=VMEM,
        scratch_shapes=[pltpu.VMEM((MEMBERS, NB * NOBS + MEMBERS), jnp.float32)],
        compiler_params=pltpu.CompilerParams(vmem_limit_bytes=32 << 20),
        name="analysis",
    )(counts, obs, *parts)


def update_kernel(mix_ref, *refs):
    parts, out_ref, state, sems = refs[:8], refs[8], refs[9], refs[10]
    members = out_ref.shape[0]
    copies = [
        pltpu.make_async_copy(parts[k], state.at[pl.ds(k * members, members)], sems.at[k]) for k in range(8)
    ]
    for copy in copies:
        copy.start()
    for copy in copies:
        copy.wait()
    out_ref[...] = dot(mix_ref[...], state[...])


def update(mix, parts):
    members, cells = parts[0].shape
    return pl.pallas_call(
        update_kernel,
        out_shape=jax.ShapeDtypeStruct((members, cells), jnp.float32),
        in_specs=[VMEM] + [ANY] * 8,
        out_specs=VMEM,
        scratch_shapes=[pltpu.VMEM((MEMBERS, cells), jnp.float32), pltpu.SemaphoreType.DMA((8,))],
        compiler_params=pltpu.CompilerParams(vmem_limit_bytes=32 << 20),
        name="update",
    )(mix, *parts)


def shift_x(k):
    return [(8 * x + r, 8 * ((x + k) % 4) + r) for x in range(4) for r in range(8)]


def shift_y(k):
    return [(8 * x + 2 * y + c, 8 * x + 2 * ((y + k) % 4) + c) for x in range(4) for y in range(4) for c in range(2)]


def shift_z(k):
    return [(z, (z + k) % 8) for z in range(8)]


SWAP = [(i, i ^ 1) for i in range(32)]


def shards(ensemble, weights, blocks, owner_ids, counts, obs_values, obs_error):
    members = ensemble.shape[0]
    cell = lax.axis_index("cell").astype(jnp.int32)
    place = jnp.concatenate([cell[None], owner_ids])
    total = local_priors(place, ensemble, weights, blocks, obs_values, obs_error)
    for shift in (shift_x, shift_y):
        near, across, far = [lax.ppermute(total, "cell", shift(k)) for k in (1, 2, 3)]
        total = (total + across) + (near + far)
    total = total + lax.ppermute(total, "cell", SWAP)
    own = total[:members]
    priors = [own] + [lax.ppermute(own, "mem", shift_z(k)) for k in range(1, 8)]
    states = [ensemble] + [lax.ppermute(ensemble, "mem", shift_z(k)) for k in range(1, 8)]
    mix = analysis(counts, total[members:], priors)
    return update(mix, states)


def solution(mesh):
    return jax.shard_map(
        shards,
        mesh=mesh,
        in_specs=(P("mem", "cell"), P(), P(), P(), P(), P("cell", None), P("cell", None)),
        out_specs=P("mem", "cell"),
        check_vma=False,
    )
```

```python
import jax
import jax.numpy as jnp
from jax import lax
from jax.experimental import pallas as pl
from jax.experimental.pallas import tpu as pltpu
from jax.sharding import PartitionSpec as P

MEMBERS = 256
NOBS = 128
NB = 4
FB = 8
BLK = 64
LANES = 128
SUB = 8
HIGH = lax.Precision.HIGHEST
VMEM = pl.BlockSpec(memory_space=pltpu.VMEM)
SMEM = pl.BlockSpec(memory_space=pltpu.SMEM)


def dot(a, b, ca=1, cb=0):
    return lax.dot_general(a, b, (((ca,), (cb,)), ((), ())), precision=HIGH)


def priors_kernel(place_ref, state_ref, weights_ref, blocks_ref, values_ref, error_ref, out_ref, operator, parts, groups):
    step = pl.program_id(0)
    members, cells = state_ref.shape
    rows = operator.shape[0]
    first = place_ref[0] * (cells // BLK)
    half = lax.broadcasted_iota(jnp.int32, (rows, LANES), 1) // BLK
    block = blocks_ref[...] - first
    for f in range(FB):
        pair = weights_ref[:, (f // 2) * LANES : (f // 2 + 1) * LANES]
        both = jnp.where(half == f % 2, pair, pltpu.roll(pair, BLK, 1))
        index = jnp.broadcast_to(block[:, f : f + 1], (rows, LANES))
        parts[f] = jnp.where((index & 1) == half, both, 0.0)
        groups[f] = index >> 1

    def tile(i, carry):
        at = pl.multiple_of(i * SUB, SUB)
        part = [parts[f, pl.ds(at, SUB), :] for f in range(FB)]
        group = [groups[f, pl.ds(at, SUB), :] for f in range(FB)]
        for g in range(cells // LANES):
            kept = [jnp.where(group[f] == g, part[f], 0.0) for f in range(FB)]
            operator[pl.ds(at, SUB), g * LANES : (g + 1) * LANES] = tree(kept)
        return carry

    lax.fori_loop(0, rows // SUB, tile, 0, unroll=2)
    out_ref[:members, :] = dot(state_ref[...], operator[...], 1, 1)
    out_ref[members:, :] = jnp.zeros((SUB, rows), jnp.float32)
    for i in range(rows // NOBS):
        batch = step * (rows // NOBS) + i
        mine = place_ref[1 + batch] == place_ref[0]
        at = slice(i * NOBS, (i + 1) * NOBS)
        out_ref[members : members + 1, at] = jnp.where(mine, values_ref[pl.ds(batch, 1), :], 0.0)
        out_ref[members + 1 : members + 2, at] = jnp.where(mine, error_ref[pl.ds(batch, 1), :], 0.0)


def local_priors(place, state, weights, blocks, values, error):
    members, cells = state.shape
    rows = 2 * NOBS
    return pl.pallas_call(
        priors_kernel,
        grid=(NB * NOBS // rows,),
        out_shape=jax.ShapeDtypeStruct((members + SUB, NB * NOBS), jnp.float32),
        in_specs=[
            SMEM,
            pl.BlockSpec((members, cells), lambda b: (0, 0)),
            pl.BlockSpec((rows, FB * BLK), lambda b: (b, 0)),
            pl.BlockSpec((rows, FB), lambda b: (b, 0)),
            pl.BlockSpec((NB, NOBS), lambda b: (0, 0)),
            pl.BlockSpec((NB, NOBS), lambda b: (0, 0)),
        ],
        out_specs=pl.BlockSpec((members + SUB, rows), lambda b: (0, b)),
        scratch_shapes=[
            pltpu.VMEM((rows, cells), jnp.float32),
            pltpu.VMEM((FB, rows, LANES), jnp.float32),
            pltpu.VMEM((FB, rows, LANES), jnp.int32),
        ],
        compiler_params=pltpu.CompilerParams(vmem_limit_bytes=40 << 20),
        name="priors",
    )(place, state, weights.reshape(NB * NOBS, FB * BLK), blocks.reshape(NB * NOBS, FB), values, error)


def spread(tile, s):
    return jnp.broadcast_to(tile[s : s + 1, :], (SUB, LANES))


def tree(terms):
    while len(terms) > 1:
        terms = [a + b for a, b in zip(terms[::2], terms[1::2])] + terms[len(terms) & ~1 :]
    return terms[0]


def eliminate(cov, noise):
    tiles = NOBS // SUB
    sub = lax.broadcasted_iota(jnp.int32, (SUB, LANES), 0)
    lane = lax.broadcasted_iota(jnp.int32, (SUB, LANES), 1)
    noise_cols = jnp.broadcast_to(noise, (NOBS, LANES)).T
    r = [cov[i * SUB : (i + 1) * SUB, :] for i in range(tiles)]
    z = [jnp.where(lane == sub + i * SUB, 1.0, 0.0) for i in range(tiles)]
    y = list(z)
    for k in range(tiles):
        rk, zk, yk = r[k], z[k], y[k]
        cols = {
            i: [jnp.broadcast_to(r[i][:, k * SUB + j : k * SUB + j + 1], (SUB, LANES)) for j in range(SUB)]
            for i in range(k, min(tiles, k + 1 + 2))
        }
        diag = cols.pop(k)
        inv = jnp.zeros((SUB, LANES), jnp.float32)
        size = jnp.zeros((SUB, LANES), jnp.float32)
        lower = []
        for j in range(SUB):
            pivot = spread(diag[j], j)
            recip = 1.0 / pivot
            inv = jnp.where(sub == j, recip, inv)
            size = jnp.where(sub == j, pivot, size)
            if j < SUB - 1:
                f = jnp.where(sub > j, diag[j] * recip, 0.0)
                lower.append(f)
                for m in range(j + 1, SUB):
                    diag[m] = diag[m] - f * spread(diag[m], j)
                rk = rk - f * spread(rk, j)
                zk = zk - f * spread(zk, j)
        root = lax.rsqrt(size)
        length = size * root
        shifted = 1.0 / (length + noise_cols[k * SUB : (k + 1) * SUB, :])
        for j in range(SUB - 1):
            yk = yk - (lower[j] * spread(length, j)) * (spread(yk, j) * spread(shifted, j))
        z[k] = zk * root
        y[k] = yk * shifted
        if k == tiles - 1:
            break
        upper = [None] + [jnp.where(sub < m, diag[m] * inv, 0.0) for m in range(1, SUB)]
        q, qz, qy = rk * inv, zk * inv, y[k] * root
        for m in range(SUB - 1, 0, -1):
            q = q - upper[m] * spread(q, m)
            qz = qz - upper[m] * spread(qz, m)
            qy = qy - upper[m] * spread(qy, m)
        rows = [[spread(v, j) for j in range(SUB)] for v in (q, qz, qy)]
        for i in cols:
            r[i] = r[i] - tree([c * w for c, w in zip(cols[i], rows[0])])
            z[i] = z[i] - tree([c * w for c, w in zip(cols[i], rows[1])])
            y[i] = y[i] - tree([c * w for c, w in zip(cols[i], rows[2])])
        first = k + 1 + 2
        if first < tiles:
            far = jnp.concatenate(r[first:], 0)[:, k * SUB : (k + 1) * SUB]
            change = jnp.dot(far, jnp.concatenate([q, qz, qy], 1), precision=lax.Precision.HIGHEST)
            for i in range(first, tiles):
                part = change[(i - first) * SUB : (i - first + 1) * SUB]
                r[i] = r[i] - part[:, :LANES]
                z[i] = z[i] - part[:, LANES : 2 * LANES]
                y[i] = y[i] - part[:, 2 * LANES :]
    return jnp.concatenate(z, 0), jnp.concatenate(y, 0)


def analysis_kernel(counts_ref, place_ref, obs_ref, *refs):
    members = MEMBERS // 8
    parts, out_ref, state = refs[:8], refs[8], refs[9]
    for k in range(8):
        state[k * members : (k + 1) * members, : NB * NOBS] = parts[k][...]
    wide = NB * NOBS + MEMBERS
    eye = lax.broadcasted_iota(jnp.int32, (MEMBERS, MEMBERS), 0) == lax.broadcasted_iota(
        jnp.int32, (MEMBERS, MEMBERS), 1
    )
    state[:, NB * NOBS :] = jnp.where(eye, 1.0, 0.0)
    lanes = lax.broadcasted_iota(jnp.int32, (1, LANES), 1)
    diagonal = lax.broadcasted_iota(jnp.int32, (NOBS, LANES), 0) == lax.broadcasted_iota(
        jnp.int32, (NOBS, LANES), 1
    )
    scale = 1.0 / (MEMBERS - 1)
    for b in range(NB):
        here = slice(b * NOBS, (b + 1) * NOBS)
        live = lanes < counts_ref[b]
        priors = state[:, here]
        mean = jnp.sum(priors, 0, keepdims=True) * (1.0 / MEMBERS)
        pert = jnp.where(live, priors - mean, 0.0)
        innovation = jnp.where(live, obs_ref[0:1, here] - mean, 0.0)
        noise = jnp.where(live, obs_ref[1:2, here], 1.0)
        pert_t = pert.T
        cov = dot(pert_t, pert) * scale + jnp.where(diagonal, noise * noise, 0.0)
        crossed = dot(pert_t, state[:, (b + 1) * NOBS :])
        inv_l, inv_ld = eliminate(cov, noise)
        half = dot(inv_l, crossed)
        solved = dot(innovation, inv_l, 1, 1)
        if b < NB - 1:
            gain = (solved - dot(pert, inv_ld, 1, 1)) * scale
            state[:, (b + 1) * NOBS :] = state[:, (b + 1) * NOBS :] + dot(gain, half)
        else:
            gain = (solved - dot(pert[:members], inv_ld, 1, 1)) * scale
            mix = state[:members, NB * NOBS : wide] + dot(gain, half)
            out_ref[...] = pltpu.roll(mix, place_ref[0] * members, 1)


def analysis(counts, place, obs, parts):
    members = MEMBERS // 8
    return pl.pallas_call(
        analysis_kernel,
        out_shape=jax.ShapeDtypeStruct((members, MEMBERS), jnp.float32),
        in_specs=[SMEM, SMEM, VMEM] + [VMEM] * 8,
        out_specs=VMEM,
        scratch_shapes=[pltpu.VMEM((MEMBERS, NB * NOBS + MEMBERS), jnp.float32)],
        compiler_params=pltpu.CompilerParams(vmem_limit_bytes=32 << 20),
        name="analysis",
    )(counts, place, obs, *parts)


def update_kernel(mix_ref, state_ref, out_ref):
    out_ref[...] = dot(mix_ref[...], state_ref[...])


def update(mix, states):
    members, cells = mix.shape[0], states.shape[1]
    return pl.pallas_call(
        update_kernel,
        out_shape=jax.ShapeDtypeStruct((members, cells), jnp.float32),
        in_specs=[VMEM, VMEM],
        out_specs=VMEM,
        compiler_params=pltpu.CompilerParams(vmem_limit_bytes=32 << 20),
        name="update",
    )(mix, states)


def shift_x(k):
    return [(8 * x + r, 8 * ((x + k) % 4) + r) for x in range(4) for r in range(8)]


def shift_y(k):
    return [(8 * x + 2 * y + c, 8 * x + 2 * ((y + k) % 4) + c) for x in range(4) for y in range(4) for c in range(2)]


def shift_z(k):
    return [((z + k) % 8, z) for z in range(8)]


SWAP = [(i, i ^ 1) for i in range(32)]


def shards(ensemble, weights, blocks, owner_ids, counts, obs_values, obs_error):
    members = ensemble.shape[0]
    cell = lax.axis_index("cell").astype(jnp.int32)
    place = jnp.concatenate([cell[None], owner_ids])
    states = lax.all_gather(ensemble, "mem", axis=0, tiled=True)
    total = local_priors(place, ensemble, weights, blocks, obs_values, obs_error)
    for shift in (shift_x, shift_y):
        near, across, far = [lax.ppermute(total, "cell", shift(k)) for k in (1, 2, 3)]
        total = (total + across) + (near + far)
    total = total + lax.ppermute(total, "cell", SWAP)
    own = total[:members]
    priors = [own] + [lax.ppermute(own, "mem", shift_z(k)) for k in range(1, 8)]
    mix = analysis(counts, lax.axis_index("mem").astype(jnp.int32)[None], total[members:], priors)
    return update(mix, states)


def solution(mesh):
    return jax.shard_map(
        shards,
        mesh=mesh,
        in_specs=(P("mem", "cell"), P(), P(), P(), P(), P("cell", None), P("cell", None)),
        out_specs=P("mem", "cell"),
        check_vma=False,
    )
```

```python
import jax
import jax.numpy as jnp
from jax import lax
from jax.experimental import pallas as pl
from jax.experimental.pallas import tpu as pltpu
from jax.sharding import PartitionSpec as P

MEMBERS = 256
NOBS = 128
NB = 4
FB = 8
BLK = 64
LANES = 128
SUB = 8
HIGH = lax.Precision.HIGHEST
HBM = pl.BlockSpec(memory_space=pltpu.HBM)
VMEM = pl.BlockSpec(memory_space=pltpu.VMEM)
SMEM = pl.BlockSpec(memory_space=pltpu.SMEM)


def dot(a, b, ca=1, cb=0):
    return lax.dot_general(a, b, (((ca,), (cb,)), ((), ())), precision=HIGH)


def split(array):
    high = array.astype(jnp.bfloat16)
    return high, (array - high.astype(jnp.float32)).astype(jnp.bfloat16)


def priors_kernel(owners_ref, state_ref, weights_ref, blocks_ref, values_ref, error_ref, out_ref):
    members, cells = state_ref.shape
    chunks = cells // LANES
    fit = LANES // members
    rows = NB * NOBS
    cell = lax.axis_index("cell")
    half = lax.broadcasted_iota(jnp.int32, (rows, LANES), 1) // BLK
    place = lax.broadcasted_iota(jnp.int32, (rows, LANES), 1) // members
    state = jnp.concatenate([state_ref[:, g * LANES : (g + 1) * LANES] for g in range(chunks)], 0)
    high, low = split(state.T)
    right = jnp.concatenate([high, high, low, low], 0)
    weights = weights_ref[...].reshape(rows, FB * BLK)
    first = cell * (cells // BLK)
    block = jnp.concatenate([(blocks_ref[b] - first).T for b in range(NB)], 0)
    total = [jnp.zeros((rows, LANES), jnp.float32) for _ in range(chunks // fit)]
    for f in range(FB):
        pair = weights[:, (f // 2) * LANES : (f // 2 + 1) * LANES]
        both = jnp.where(half == f % 2, pair, pltpu.roll(pair, BLK, 1))
        index = jnp.broadcast_to(block[:, f : f + 1], (rows, LANES))
        high, low = split(jnp.where((index & 1) == half, both, 0.0))
        left = jnp.concatenate([high, low, high, low], 1)
        product = jnp.dot(left, right, preferred_element_type=jnp.float32)
        group = (index >> 1) - place
        for c in range(chunks // fit):
            total[c] = total[c] + jnp.where(group == c * fit, product[:, c * LANES : (c + 1) * LANES], 0.0)
    kept = tree(total)
    shift = LANES // 2
    while shift >= members:
        kept = kept + pltpu.roll(kept, shift, 1)
        shift //= 2
    for b in range(NB):
        at = slice(b * NOBS, (b + 1) * NOBS)
        mine = owners_ref[b] == cell
        out_ref[:members, at] = kept[at].T[:members]
        out_ref[members : members + 1, at] = jnp.where(mine, values_ref[b : b + 1, :], 0.0)
        out_ref[members + 1 : members + 2, at] = jnp.where(mine, error_ref[b : b + 1, :], 0.0)
    out_ref[members + 2 :, :] = jnp.zeros((SUB - 2, rows), jnp.float32)


def local_priors(owners, state, weights, blocks, values, error):
    members = state.shape[0]
    return pl.pallas_call(
        priors_kernel,
        out_shape=jax.ShapeDtypeStruct((members + SUB, NB * NOBS), jnp.float32),
        in_specs=[SMEM] + [VMEM] * 5,
        out_specs=VMEM,
        compiler_params=pltpu.CompilerParams(vmem_limit_bytes=60 << 20),
        name="priors",
    )(owners, state, weights, blocks.transpose(0, 2, 1), values, error)


def spread(tile, s):
    return jnp.broadcast_to(tile[s : s + 1, :], (SUB, LANES))


def tree(terms):
    while len(terms) > 1:
        terms = [a + b for a, b in zip(terms[::2], terms[1::2])] + terms[len(terms) & ~1 :]
    return terms[0]


def eliminate(cov, noise):
    tiles = NOBS // SUB
    sub = lax.broadcasted_iota(jnp.int32, (SUB, LANES), 0)
    lane = lax.broadcasted_iota(jnp.int32, (SUB, LANES), 1)
    noise_cols = jnp.broadcast_to(noise, (NOBS, LANES)).T
    r = [cov[i * SUB : (i + 1) * SUB, :] for i in range(tiles)]
    z = [jnp.where(lane == sub + i * SUB, 1.0, 0.0) for i in range(tiles)]
    y = list(z)
    for k in range(tiles):
        rk, zk, yk = r[k], z[k], y[k]
        cols = {
            i: [jnp.broadcast_to(r[i][:, k * SUB + j : k * SUB + j + 1], (SUB, LANES)) for j in range(SUB)]
            for i in range(k, min(tiles, k + 1 + 2))
        }
        diag = cols.pop(k)
        inv = jnp.zeros((SUB, LANES), jnp.float32)
        size = jnp.zeros((SUB, LANES), jnp.float32)
        lower = []
        for j in range(SUB):
            pivot = spread(diag[j], j)
            recip = 1.0 / pivot
            inv = jnp.where(sub == j, recip, inv)
            size = jnp.where(sub == j, pivot, size)
            if j < SUB - 1:
                f = jnp.where(sub > j, diag[j] * recip, 0.0)
                lower.append(f)
                for m in range(j + 1, SUB):
                    diag[m] = diag[m] - f * spread(diag[m], j)
                rk = rk - f * spread(rk, j)
                zk = zk - f * spread(zk, j)
        root = lax.rsqrt(size)
        length = size * root
        shifted = 1.0 / (length + noise_cols[k * SUB : (k + 1) * SUB, :])
        for j in range(SUB - 1):
            yk = yk - (lower[j] * spread(length, j)) * (spread(yk, j) * spread(shifted, j))
        z[k] = zk * root
        y[k] = yk * shifted
        if k == tiles - 1:
            break
        upper = [None] + [jnp.where(sub < m, diag[m] * inv, 0.0) for m in range(1, SUB)]
        q, qz, qy = rk * inv, zk * inv, y[k] * root
        for m in range(SUB - 1, 0, -1):
            q = q - upper[m] * spread(q, m)
            qz = qz - upper[m] * spread(qz, m)
            qy = qy - upper[m] * spread(qy, m)
        rows = [[spread(v, j) for j in range(SUB)] for v in (q, qz, qy)]
        for i in cols:
            r[i] = r[i] - tree([c * w for c, w in zip(cols[i], rows[0])])
            z[i] = z[i] - tree([c * w for c, w in zip(cols[i], rows[1])])
            y[i] = y[i] - tree([c * w for c, w in zip(cols[i], rows[2])])
        first = k + 1 + 2
        if first < tiles:
            far = jnp.concatenate(r[first:], 0)[:, k * SUB : (k + 1) * SUB]
            change = jnp.dot(far, jnp.concatenate([q, qz, qy], 1), precision=lax.Precision.HIGHEST)
            for i in range(first, tiles):
                part = change[(i - first) * SUB : (i - first + 1) * SUB]
                r[i] = r[i] - part[:, :LANES]
                z[i] = z[i] - part[:, LANES : 2 * LANES]
                y[i] = y[i] - part[:, 2 * LANES :]
    return jnp.concatenate(z, 0), jnp.concatenate(y, 0)


def analysis_kernel(counts_ref, obs_ref, *refs):
    members = MEMBERS // 8
    parts, out_ref, state = refs[:8], refs[8], refs[9]
    for k in range(8):
        state[k * members : (k + 1) * members, : NB * NOBS] = parts[k][...]
    wide = NB * NOBS + MEMBERS
    eye = lax.broadcasted_iota(jnp.int32, (MEMBERS, MEMBERS), 0) == lax.broadcasted_iota(
        jnp.int32, (MEMBERS, MEMBERS), 1
    )
    state[:, NB * NOBS :] = jnp.where(eye, 1.0, 0.0)
    lanes = lax.broadcasted_iota(jnp.int32, (1, LANES), 1)
    diagonal = lax.broadcasted_iota(jnp.int32, (NOBS, LANES), 0) == lax.broadcasted_iota(
        jnp.int32, (NOBS, LANES), 1
    )
    scale = 1.0 / (MEMBERS - 1)
    for b in range(NB):
        here = slice(b * NOBS, (b + 1) * NOBS)
        live = lanes < counts_ref[b]
        priors = state[:, here]
        mean = jnp.sum(priors, 0, keepdims=True) * (1.0 / MEMBERS)
        pert = jnp.where(live, priors - mean, 0.0)
        innovation = jnp.where(live, obs_ref[0:1, here] - mean, 0.0)
        noise = jnp.where(live, obs_ref[1:2, here], 1.0)
        pert_t = pert.T
        cov = dot(pert_t, pert) * scale + jnp.where(diagonal, noise * noise, 0.0)
        crossed = dot(pert_t, state[:, (b + 1) * NOBS :])
        inv_l, inv_ld = eliminate(cov, noise)
        half = dot(inv_l, crossed)
        solved = dot(innovation, inv_l, 1, 1)
        if b < NB - 1:
            gain = (solved - dot(pert, inv_ld, 1, 1)) * scale
            state[:, (b + 1) * NOBS :] = state[:, (b + 1) * NOBS :] + dot(gain, half)
        else:
            gain = (solved - dot(pert[:members], inv_ld, 1, 1)) * scale
            out_ref[...] = state[:members, NB * NOBS : wide] + dot(gain, half)


def analysis(counts, obs, parts):
    members = MEMBERS // 8
    return pl.pallas_call(
        analysis_kernel,
        out_shape=jax.ShapeDtypeStruct((members, MEMBERS), jnp.float32),
        in_specs=[SMEM, VMEM] + [VMEM] * 8,
        out_specs=VMEM,
        scratch_shapes=[pltpu.VMEM((MEMBERS, NB * NOBS + MEMBERS), jnp.float32)],
        compiler_params=pltpu.CompilerParams(vmem_limit_bytes=32 << 20),
        name="analysis",
    )(counts, obs, *parts)


def update_kernel(mix_ref, *refs):
    parts, out_ref, state, sems = refs[:8], refs[8], refs[9], refs[10]
    members = out_ref.shape[0]
    copies = [
        pltpu.make_async_copy(parts[k], state.at[pl.ds(k * members, members)], sems.at[k]) for k in range(8)
    ]
    for copy in copies:
        copy.start()
    for copy in copies:
        copy.wait()
    out_ref[...] = dot(mix_ref[...], state[...])


def update(mix, parts):
    members, cells = parts[0].shape
    return pl.pallas_call(
        update_kernel,
        out_shape=jax.ShapeDtypeStruct((members, cells), jnp.float32),
        in_specs=[VMEM] + [HBM] * 8,
        out_specs=VMEM,
        scratch_shapes=[pltpu.VMEM((MEMBERS, cells), jnp.float32), pltpu.SemaphoreType.DMA((8,))],
        compiler_params=pltpu.CompilerParams(vmem_limit_bytes=32 << 20),
        name="update",
    )(mix, *parts)


def nothing(array):
    return jnp.minimum(jnp.abs(array[:1, :1]), 0.0)


def shift_x(k):
    return [(8 * x + r, 8 * ((x + k) % 4) + r) for x in range(4) for r in range(8)]


def shift_y(k):
    return [(8 * x + 2 * y + c, 8 * x + 2 * ((y + k) % 4) + c) for x in range(4) for y in range(4) for c in range(2)]


def shift_z(k):
    return [((z + k) % 8, z) for z in range(8)]


SWAP = [(i, i ^ 1) for i in range(32)]


def shards(ensemble, weights, blocks, owner_ids, counts, obs_values, obs_error):
    members = ensemble.shape[0]
    total = local_priors(owner_ids, ensemble, weights, blocks, obs_values, obs_error)
    up, down = [ensemble], [ensemble]

    def ring():
        up.append(lax.ppermute(up[-1], "mem", shift_z(1)))
        down.append(lax.ppermute(down[-1], "mem", shift_z(7)))
        return nothing(up[-1]) + nothing(down[-1])

    for shift in (shift_x, shift_y):
        near, across, far = [lax.ppermute(total, "cell", shift(k)) for k in (1, 2, 3)]
        total = (total + across) + (near + far) + ring()
    total = total + lax.ppermute(total, "cell", SWAP)
    own = total[:members]
    priors = [own] + [lax.ppermute(own, "mem", shift_z(k)) for k in range(1, 8)]
    obs = total[members:] + ring()
    middle = lax.ppermute(up[-1], "mem", shift_z(1))
    mix = analysis(counts, obs, priors)
    return update(mix, up + [middle] + down[:0:-1])


def solution(mesh):
    return jax.shard_map(
        shards,
        mesh=mesh,
        in_specs=(P("mem", "cell"), P(), P(), P(), P(), P("cell", None), P("cell", None)),
        out_specs=P("mem", "cell"),
        check_vma=False,
    )
```

```python
import jax
import jax.numpy as jnp
from jax import lax
from jax.experimental import pallas as pl
from jax.experimental.pallas import tpu as pltpu
from jax.sharding import PartitionSpec as P

MEMBERS = 256
NOBS = 128
NB = 4
FB = 8
BLK = 64
LANES = 128
SUB = 8
HIGH = lax.Precision.HIGHEST
HBM = pl.BlockSpec(memory_space=pltpu.HBM)
VMEM = pl.BlockSpec(memory_space=pltpu.VMEM)
SMEM = pl.BlockSpec(memory_space=pltpu.SMEM)


def dot(a, b, ca=1, cb=0):
    return lax.dot_general(a, b, (((ca,), (cb,)), ((), ())), precision=HIGH)


def split(array):
    high = array.astype(jnp.bfloat16)
    return high, (array - high.astype(jnp.float32)).astype(jnp.bfloat16)


def priors_kernel(owners_ref, state_ref, weights_ref, blocks_ref, values_ref, error_ref, out_ref):
    members, cells = state_ref.shape
    chunks = cells // LANES
    fit = LANES // members
    rows = NB * NOBS
    cell = lax.axis_index("cell")
    half = lax.broadcasted_iota(jnp.int32, (rows, LANES), 1) // BLK
    place = lax.broadcasted_iota(jnp.int32, (rows, LANES), 1) // members
    state = jnp.concatenate([state_ref[:, g * LANES : (g + 1) * LANES] for g in range(chunks)], 0)
    high, low = split(state.T)
    right = jnp.concatenate([high, high, low, low], 0)
    weights = weights_ref[...].reshape(rows, FB * BLK)
    first = cell * (cells // BLK)
    block = jnp.concatenate([(blocks_ref[b] - first).T for b in range(NB)], 0)
    total = [jnp.zeros((rows, LANES), jnp.float32) for _ in range(chunks // fit)]
    for f in range(FB):
        pair = weights[:, (f // 2) * LANES : (f // 2 + 1) * LANES]
        both = jnp.where(half == f % 2, pair, pltpu.roll(pair, BLK, 1))
        index = jnp.broadcast_to(block[:, f : f + 1], (rows, LANES))
        high, low = split(jnp.where((index & 1) == half, both, 0.0))
        left = jnp.concatenate([high, low, high, low], 1)
        product = jnp.dot(left, right, preferred_element_type=jnp.float32)
        group = (index >> 1) - place
        for c in range(chunks // fit):
            total[c] = total[c] + jnp.where(group == c * fit, product[:, c * LANES : (c + 1) * LANES], 0.0)
    kept = tree(total)
    shift = LANES // 2
    while shift >= members:
        kept = kept + pltpu.roll(kept, shift, 1)
        shift //= 2
    for b in range(NB):
        at = slice(b * NOBS, (b + 1) * NOBS)
        mine = owners_ref[b] == cell
        out_ref[:members, at] = kept[at].T[:members]
        out_ref[members : members + 1, at] = jnp.where(mine, values_ref[b : b + 1, :], 0.0)
        out_ref[members + 1 : members + 2, at] = jnp.where(mine, error_ref[b : b + 1, :], 0.0)
    out_ref[members + 2 :, :] = jnp.zeros((SUB - 2, rows), jnp.float32)


def local_priors(owners, state, weights, blocks, values, error):
    members = state.shape[0]
    return pl.pallas_call(
        priors_kernel,
        out_shape=jax.ShapeDtypeStruct((members + SUB, NB * NOBS), jnp.float32),
        in_specs=[SMEM] + [VMEM] * 5,
        out_specs=VMEM,
        compiler_params=pltpu.CompilerParams(vmem_limit_bytes=60 << 20),
        name="priors",
    )(owners, state, weights, blocks.transpose(0, 2, 1), values, error)


def spread(tile, s):
    return jnp.broadcast_to(tile[s : s + 1, :], (SUB, LANES))


def tree(terms):
    while len(terms) > 1:
        terms = [a + b for a, b in zip(terms[::2], terms[1::2])] + terms[len(terms) & ~1 :]
    return terms[0]


def split3(a):
    h = a.astype(jnp.bfloat16)
    rest = a - h.astype(jnp.float32)
    m = rest.astype(jnp.bfloat16)
    return h, m, (rest - m.astype(jnp.float32)).astype(jnp.bfloat16)


def eliminate(cov, noise):
    tiles = NOBS // SUB
    sub = lax.broadcasted_iota(jnp.int32, (SUB, LANES), 0)
    lane = lax.broadcasted_iota(jnp.int32, (SUB, LANES), 1)
    noise_cols = jnp.broadcast_to(noise, (NOBS, LANES)).T
    r = [cov[i * SUB : (i + 1) * SUB, :] for i in range(tiles)]
    z = [jnp.where(lane == sub + i * SUB, 1.0, 0.0) for i in range(tiles)]
    y = list(z)
    for k in range(tiles):
        rk, zk, yk = r[k], z[k], y[k]
        cols = {
            i: [jnp.broadcast_to(r[i][:, k * SUB + j : k * SUB + j + 1], (SUB, LANES)) for j in range(SUB)]
            for i in range(k, min(tiles, k + 1 + 1))
        }
        diag = cols.pop(k)
        zero = jnp.zeros((SUB, LANES), jnp.float32)
        root, length, z[k] = zero, zero, zero
        upper = [zero] * SUB
        lower = []
        for j in range(0, SUB, 2):
            one, two = sub == j, sub == j + 1
            a, b, d = spread(diag[j], j), spread(diag[j], j + 1), spread(diag[j + 1], j + 1)
            det = a * d - b * b
            recip = 1.0 / det
            root_a = lax.rsqrt(a)
            ratio = b * (root_a * root_a)
            root_b = a * root_a * lax.rsqrt(det)
            length_b = det * (root_a * root_a) * root_b
            root = jnp.where(one, root_a, jnp.where(two, root_b, root))
            length = jnp.where(one, a * root_a, jnp.where(two, length_b, length))
            lower.append(jnp.where(sub > j, diag[j] * root_a, 0.0))
            lower.append(jnp.where(sub > j + 1, (diag[j + 1] - diag[j] * ratio) * root_b, 0.0))
            z[k] = jnp.where(one, zk * root_a, jnp.where(two, (zk - ratio * spread(zk, j)) * root_b, z[k]))
            if k == tiles - 1 and j == SUB - 2:
                continue
            upper[j + 1] = jnp.where(one, b * root_a, upper[j + 1])
            for m in range(j + 2, SUB):
                second = (diag[m] - ratio * spread(diag[m], j)) * root_b
                upper[m] = jnp.where(one, diag[m] * root_a, jnp.where(two, second, upper[m]))
            left = jnp.where(one, -1.0, jnp.where(two, 0.0, diag[j]))
            right = jnp.where(two, -1.0, jnp.where(one, 0.0, diag[j + 1]))

            def reduce(v):
                p, q = spread(v, j), spread(v, j + 1)
                return jnp.where(one | two, 0.0, v) - (left * (d * p - b * q) + right * (a * q - b * p)) * recip

            for m in range(j + 2, SUB):
                diag[m] = reduce(diag[m])
            rk, zk = reduce(rk), reduce(zk)
        shifted = 1.0 / (length + noise_cols[k * SUB : (k + 1) * SUB, :])
        for j in range(SUB - 1):
            yk = yk - lower[j] * (spread(yk, j) * spread(shifted, j))
        y[k] = yk * shifted
        if k == tiles - 1:
            break
        q, qz, qy = rk, zk, y[k]
        for m in range(SUB - 1, 0, -1):
            qy = qy - upper[m] * (spread(qy, m) * spread(root, m))
        qy = qy * root
        rows = [[spread(v, j) for j in range(SUB)] for v in (q, qz, qy)]
        for i in cols:
            r[i] = r[i] - tree([c * w for c, w in zip(cols[i], rows[0])])
            z[i] = z[i] - tree([c * w for c, w in zip(cols[i], rows[1])])
            y[i] = y[i] - tree([c * w for c, w in zip(cols[i], rows[2])])
        first = k + 1 + 1
        if first < tiles:
            far = jnp.concatenate(r[first:], 0)[:, k * SUB : (k + 1) * SUB]
            change = jnp.concatenate([q, qz, qy], 1)
            f0, f1, f2 = split3(far)
            c0, c1, c2 = split3(change)
            left = jnp.concatenate([f0, f1, f0, f1, f2, f0], 1)
            right = jnp.concatenate([c0, c0, c1, c1, c0, c2], 0)
            change = jnp.dot(left, right, preferred_element_type=jnp.float32)
            for i in range(first, tiles):
                part = change[(i - first) * SUB : (i - first + 1) * SUB]
                r[i] = r[i] - part[:, :LANES]
                z[i] = z[i] - part[:, LANES : 2 * LANES]
                y[i] = y[i] - part[:, 2 * LANES :]
    return jnp.concatenate(z, 0), jnp.concatenate(y, 0)


def analysis_kernel(counts_ref, obs_ref, *refs):
    members = MEMBERS // 8
    parts, out_ref, state = refs[:8], refs[8], refs[9]
    for k in range(8):
        state[k * members : (k + 1) * members, : NB * NOBS] = parts[k][...]
    wide = NB * NOBS + MEMBERS
    eye = lax.broadcasted_iota(jnp.int32, (MEMBERS, MEMBERS), 0) == lax.broadcasted_iota(
        jnp.int32, (MEMBERS, MEMBERS), 1
    )
    state[:, NB * NOBS :] = jnp.where(eye, 1.0, 0.0)
    lanes = lax.broadcasted_iota(jnp.int32, (1, LANES), 1)
    diagonal = lax.broadcasted_iota(jnp.int32, (NOBS, LANES), 0) == lax.broadcasted_iota(
        jnp.int32, (NOBS, LANES), 1
    )
    scale = 1.0 / (MEMBERS - 1)
    for b in range(NB):
        here = slice(b * NOBS, (b + 1) * NOBS)
        live = lanes < counts_ref[b]
        priors = state[:, here]
        mean = jnp.sum(priors, 0, keepdims=True) * (1.0 / MEMBERS)
        pert = jnp.where(live, priors - mean, 0.0)
        innovation = jnp.where(live, obs_ref[0:1, here] - mean, 0.0)
        noise = jnp.where(live, obs_ref[1:2, here], 1.0)
        pert_t = pert.T
        cov = dot(pert_t, pert) * scale + jnp.where(diagonal, noise * noise, 0.0)
        crossed = dot(pert_t, state[:, (b + 1) * NOBS :])
        inv_l, inv_ld = eliminate(cov, noise)
        half = dot(inv_l, crossed)
        solved = dot(innovation, inv_l, 1, 1)
        if b < NB - 1:
            gain = (solved - dot(pert, inv_ld, 1, 1)) * scale
            state[:, (b + 1) * NOBS :] = state[:, (b + 1) * NOBS :] + dot(gain, half)
        else:
            gain = (solved - dot(pert[:members], inv_ld, 1, 1)) * scale
            out_ref[...] = state[:members, NB * NOBS : wide] + dot(gain, half)


def analysis(counts, obs, parts):
    members = MEMBERS // 8
    return pl.pallas_call(
        analysis_kernel,
        out_shape=jax.ShapeDtypeStruct((members, MEMBERS), jnp.float32),
        in_specs=[SMEM, VMEM] + [VMEM] * 8,
        out_specs=VMEM,
        scratch_shapes=[pltpu.VMEM((MEMBERS, NB * NOBS + MEMBERS), jnp.float32)],
        compiler_params=pltpu.CompilerParams(vmem_limit_bytes=32 << 20),
        name="analysis",
    )(counts, obs, *parts)


def update_kernel(mix_ref, *refs):
    parts, out_ref, state, sems = refs[:8], refs[8], refs[9], refs[10]
    members = out_ref.shape[0]
    copies = [
        pltpu.make_async_copy(parts[k], state.at[pl.ds(k * members, members)], sems.at[k]) for k in range(8)
    ]
    for copy in copies:
        copy.start()
    for copy in copies:
        copy.wait()
    out_ref[...] = dot(mix_ref[...], state[...])


def update(mix, parts):
    members, cells = parts[0].shape
    return pl.pallas_call(
        update_kernel,
        out_shape=jax.ShapeDtypeStruct((members, cells), jnp.float32),
        in_specs=[VMEM] + [HBM] * 8,
        out_specs=VMEM,
        scratch_shapes=[pltpu.VMEM((MEMBERS, cells), jnp.float32), pltpu.SemaphoreType.DMA((8,))],
        compiler_params=pltpu.CompilerParams(vmem_limit_bytes=32 << 20),
        name="update",
    )(mix, *parts)


def shift_x(k):
    return [(8 * x + r, 8 * ((x + k) % 4) + r) for x in range(4) for r in range(8)]


def shift_y(k):
    return [(8 * x + 2 * y + c, 8 * x + 2 * ((y + k) % 4) + c) for x in range(4) for y in range(4) for c in range(2)]


def shift_z(k):
    return [((z + k) % 8, z) for z in range(8)]


SWAP = [(i, i ^ 1) for i in range(32)]


def shards(ensemble, weights, blocks, owner_ids, counts, obs_values, obs_error):
    members = ensemble.shape[0]
    total = local_priors(owner_ids, ensemble, weights, blocks, obs_values, obs_error)
    up, down = [ensemble], [ensemble]

    def ring(ready):
        up.append(lax.ppermute(up[-1], "mem", shift_z(1)))
        down.append(lax.ppermute(down[-1], "mem", shift_z(7)))
        ready, up[-1], down[-1] = lax.optimization_barrier((ready, up[-1], down[-1]))
        return ready

    total = ring(total)
    for shift in (shift_x, shift_y):
        near, across, far = [lax.ppermute(total, "cell", shift(k)) for k in (1, 2, 3)]
        total = ring((total + across) + (near + far))
    middle = lax.ppermute(up[-1], "mem", shift_z(1))
    total = total + lax.ppermute(total, "cell", SWAP)
    own = total[:members]
    priors = [own] + [lax.ppermute(own, "mem", shift_z(k)) for k in range(1, 8)]
    mix = analysis(counts, total[members:], priors)
    return update(mix, up + [middle] + down[:0:-1])


def solution(mesh):
    return jax.shard_map(
        shards,
        mesh=mesh,
        in_specs=(P("mem", "cell"), P(), P(), P(), P(), P("cell", None), P("cell", None)),
        out_specs=P("mem", "cell"),
        check_vma=False,
    )
```

```python
import jax
import jax.numpy as jnp
from jax import lax
from jax.experimental import pallas as pl
from jax.experimental.pallas import tpu as pltpu
from jax.sharding import PartitionSpec as P

MEMBERS = 256
NOBS = 128
NB = 4
FB = 8
BLK = 64
LANES = 128
SUB = 8
HIGH = lax.Precision.HIGHEST
HBM = pl.BlockSpec(memory_space=pltpu.HBM)
VMEM = pl.BlockSpec(memory_space=pltpu.VMEM)
SMEM = pl.BlockSpec(memory_space=pltpu.SMEM)


def dot(a, b, ca=1, cb=0):
    return lax.dot_general(a, b, (((ca,), (cb,)), ((), ())), precision=HIGH)


def split(array):
    high = array.astype(jnp.bfloat16)
    return high, (array - high.astype(jnp.float32)).astype(jnp.bfloat16)


def priors_kernel(owners_ref, state_ref, weights_ref, blocks_ref, values_ref, error_ref, out_ref):
    members, cells = state_ref.shape
    chunks = cells // LANES
    fit = LANES // members
    rows = NB * NOBS
    cell = lax.axis_index("cell")
    half = lax.broadcasted_iota(jnp.int32, (rows, LANES), 1) // BLK
    place = lax.broadcasted_iota(jnp.int32, (rows, LANES), 1) // members
    state = jnp.concatenate([state_ref[:, g * LANES : (g + 1) * LANES] for g in range(chunks)], 0)
    high, low = split(state.T)
    right = jnp.concatenate([high, high, low, low], 0)
    weights = weights_ref[...].reshape(rows, FB * BLK)
    first = cell * (cells // BLK)
    block = jnp.concatenate([(blocks_ref[b] - first).T for b in range(NB)], 0)
    total = [jnp.zeros((rows, LANES), jnp.float32) for _ in range(chunks // fit)]
    for f in range(FB):
        pair = weights[:, (f // 2) * LANES : (f // 2 + 1) * LANES]
        both = jnp.where(half == f % 2, pair, pltpu.roll(pair, BLK, 1))
        index = jnp.broadcast_to(block[:, f : f + 1], (rows, LANES))
        high, low = split(jnp.where((index & 1) == half, both, 0.0))
        left = jnp.concatenate([high, low, high, low], 1)
        product = jnp.dot(left, right, preferred_element_type=jnp.float32)
        group = (index >> 1) - place
        for c in range(chunks // fit):
            total[c] = total[c] + jnp.where(group == c * fit, product[:, c * LANES : (c + 1) * LANES], 0.0)
    kept = tree(total)
    shift = LANES // 2
    while shift >= members:
        kept = kept + pltpu.roll(kept, shift, 1)
        shift //= 2
    for b in range(NB):
        at = slice(b * NOBS, (b + 1) * NOBS)
        mine = owners_ref[b] == cell
        out_ref[:members, at] = kept[at].T[:members]
        out_ref[members : members + 1, at] = jnp.where(mine, values_ref[b : b + 1, :], 0.0)
        out_ref[members + 1 : members + 2, at] = jnp.where(mine, error_ref[b : b + 1, :], 0.0)
    out_ref[members + 2 :, :] = jnp.zeros((SUB - 2, rows), jnp.float32)


def local_priors(owners, state, weights, blocks, values, error):
    members = state.shape[0]
    return pl.pallas_call(
        priors_kernel,
        out_shape=jax.ShapeDtypeStruct((members + SUB, NB * NOBS), jnp.float32),
        in_specs=[SMEM] + [VMEM] * 5,
        out_specs=VMEM,
        compiler_params=pltpu.CompilerParams(vmem_limit_bytes=60 << 20),
        name="priors",
    )(owners, state, weights, blocks.transpose(0, 2, 1), values, error)


def spread(tile, s):
    return jnp.broadcast_to(tile[s : s + 1, :], (SUB, LANES))


def tree(terms):
    while len(terms) > 1:
        terms = [a + b for a, b in zip(terms[::2], terms[1::2])] + terms[len(terms) & ~1 :]
    return terms[0]


def split3(a):
    h = a.astype(jnp.bfloat16)
    rest = a - h.astype(jnp.float32)
    m = rest.astype(jnp.bfloat16)
    return h, m, (rest - m.astype(jnp.float32)).astype(jnp.bfloat16)


def eliminate(cov, noise):
    tiles = NOBS // SUB
    sub = lax.broadcasted_iota(jnp.int32, (SUB, LANES), 0)
    lane = lax.broadcasted_iota(jnp.int32, (SUB, LANES), 1)
    noise_cols = jnp.broadcast_to(noise, (NOBS, LANES)).T
    r = [cov[i * SUB : (i + 1) * SUB, :] for i in range(tiles)]
    z = [jnp.where(lane == sub + i * SUB, 1.0, 0.0) for i in range(tiles)]
    y = list(z)
    for k in range(tiles):
        rk, zk, yk = r[k], z[k], y[k]
        cols = {
            i: [jnp.broadcast_to(r[i][:, k * SUB + j : k * SUB + j + 1], (SUB, LANES)) for j in range(SUB)]
            for i in range(k, min(tiles, k + 1 + 1))
        }
        diag = cols.pop(k)
        zero = jnp.zeros((SUB, LANES), jnp.float32)
        root, length, z[k] = zero, zero, zero
        upper = [zero] * SUB
        lower = []
        for j in range(0, SUB, 2):
            one, two = sub == j, sub == j + 1
            a, b, d = spread(diag[j], j), spread(diag[j], j + 1), spread(diag[j + 1], j + 1)
            det = a * d - b * b
            recip = 1.0 / det
            root_a = lax.rsqrt(a)
            ratio = b * (root_a * root_a)
            root_b = a * root_a * lax.rsqrt(det)
            length_b = det * (root_a * root_a) * root_b
            root = jnp.where(one, root_a, jnp.where(two, root_b, root))
            length = jnp.where(one, a * root_a, jnp.where(two, length_b, length))
            lower.append(jnp.where(sub > j, diag[j] * root_a, 0.0))
            lower.append(jnp.where(sub > j + 1, (diag[j + 1] - diag[j] * ratio) * root_b, 0.0))
            z[k] = jnp.where(one, zk * root_a, jnp.where(two, (zk - ratio * spread(zk, j)) * root_b, z[k]))
            if k == tiles - 1 and j == SUB - 2:
                continue
            upper[j + 1] = jnp.where(one, b * root_a, upper[j + 1])
            for m in range(j + 2, SUB):
                second = (diag[m] - ratio * spread(diag[m], j)) * root_b
                upper[m] = jnp.where(one, diag[m] * root_a, jnp.where(two, second, upper[m]))
            left = jnp.where(one, -1.0, jnp.where(two, 0.0, diag[j]))
            right = jnp.where(two, -1.0, jnp.where(one, 0.0, diag[j + 1]))

            def reduce(v):
                p, q = spread(v, j), spread(v, j + 1)
                return jnp.where(one | two, 0.0, v) - (left * (d * p - b * q) + right * (a * q - b * p)) * recip

            for m in range(j + 2, SUB):
                diag[m] = reduce(diag[m])
            rk, zk = reduce(rk), reduce(zk)
        shifted = 1.0 / (length + noise_cols[k * SUB : (k + 1) * SUB, :])
        for j in range(SUB - 1):
            yk = yk - lower[j] * (spread(yk, j) * spread(shifted, j))
        y[k] = yk * shifted
        if k == tiles - 1:
            break
        q, qz, qy = rk, zk, y[k]
        for m in range(SUB - 1, 0, -1):
            qy = qy - upper[m] * (spread(qy, m) * spread(root, m))
        qy = qy * root
        rows = [[spread(v, j) for j in range(SUB)] for v in (q, qz, qy)]
        for i in cols:
            r[i] = r[i] - tree([c * w for c, w in zip(cols[i], rows[0])])
            z[i] = z[i] - tree([c * w for c, w in zip(cols[i], rows[1])])
            y[i] = y[i] - tree([c * w for c, w in zip(cols[i], rows[2])])
        first = k + 1 + 1
        if first < tiles:
            far = jnp.concatenate(r[first:], 0)[:, k * SUB : (k + 1) * SUB]
            change = jnp.concatenate([q, qz, qy], 1)
            f0, f1, f2 = split3(far)
            c0, c1, c2 = split3(change)
            left = jnp.concatenate([f0, f1, f0, f1, f2, f0], 1)
            right = jnp.concatenate([c0, c0, c1, c1, c0, c2], 0)
            change = jnp.dot(left, right, preferred_element_type=jnp.float32)
            for i in range(first, tiles):
                part = change[(i - first) * SUB : (i - first + 1) * SUB]
                r[i] = r[i] - part[:, :LANES]
                z[i] = z[i] - part[:, LANES : 2 * LANES]
                y[i] = y[i] - part[:, 2 * LANES :]
    return jnp.concatenate(z, 0), jnp.concatenate(y, 0)


def analyse(batches, counts_ref, obs_ref, state, out_ref):
    lanes = lax.broadcasted_iota(jnp.int32, (1, LANES), 1)
    diagonal = lax.broadcasted_iota(jnp.int32, (NOBS, LANES), 0) == lax.broadcasted_iota(
        jnp.int32, (NOBS, LANES), 1
    )
    scale = 1.0 / (MEMBERS - 1)
    for at, b in enumerate(batches):
        here, rest = slice(at * NOBS, (at + 1) * NOBS), slice((at + 1) * NOBS, None)
        live = lanes < counts_ref[b]
        priors = state[:, here]
        mean = jnp.sum(priors, 0, keepdims=True) * (1.0 / MEMBERS)
        pert = jnp.where(live, priors - mean, 0.0)
        innovation = jnp.where(live, obs_ref[0:1, b * NOBS : (b + 1) * NOBS] - mean, 0.0)
        noise = jnp.where(live, obs_ref[1:2, b * NOBS : (b + 1) * NOBS], 1.0)
        pert_t = pert.T
        cov = dot(pert_t, pert) * scale + jnp.where(diagonal, noise * noise, 0.0)
        crossed = dot(pert_t, state[:, rest])
        inv_l, inv_ld = eliminate(cov, noise)
        half = dot(inv_l, crossed)
        solved = dot(innovation, inv_l, 1, 1)
        if b < NB - 1:
            gain = (solved - dot(pert, inv_ld, 1, 1)) * scale
            changed = state[:, rest] + dot(gain, half)
            if at < len(batches) - 1:
                state[:, rest] = changed
            else:
                out_ref[...] = changed
        else:
            members = out_ref.shape[0]
            gain = (solved - dot(pert[:members], inv_ld, 1, 1)) * scale
            out_ref[...] = state[:members, rest] + dot(gain, half)


EARLY, LATE = range(NB // 2), range(NB // 2, NB)


def early_kernel(counts_ref, obs_ref, *refs):
    parts, out_ref, state = refs[:8], refs[8], refs[9]
    members = MEMBERS // 8
    for k in range(8):
        state[k * members : (k + 1) * members, : NB * NOBS] = parts[k][...]
    eye = lax.broadcasted_iota(jnp.int32, (MEMBERS, MEMBERS), 0) == lax.broadcasted_iota(
        jnp.int32, (MEMBERS, MEMBERS), 1
    )
    state[:, NB * NOBS :] = jnp.where(eye, 1.0, 0.0)
    analyse(EARLY, counts_ref, obs_ref, state, out_ref)


def late_kernel(counts_ref, obs_ref, state_ref, out_ref, state):
    state[...] = state_ref[...]
    analyse(LATE, counts_ref, obs_ref, state, out_ref)


def analysis(counts, obs, arrays, batches):
    early = batches is EARLY
    wide = NB * NOBS + MEMBERS - batches[0] * NOBS
    shape = (MEMBERS, wide - len(batches) * NOBS) if early else (MEMBERS // 8, MEMBERS)
    return pl.pallas_call(
        early_kernel if early else late_kernel,
        out_shape=jax.ShapeDtypeStruct(shape, jnp.float32),
        in_specs=[SMEM] + [VMEM] * (1 + len(arrays)),
        out_specs=VMEM,
        scratch_shapes=[pltpu.VMEM((MEMBERS, wide), jnp.float32)],
        compiler_params=pltpu.CompilerParams(vmem_limit_bytes=32 << 20),
        name="early" if early else "late",
    )(counts, obs, *arrays)


def update_kernel(mix_ref, *refs):
    parts, out_ref, state, sems = refs[:8], refs[8], refs[9], refs[10]
    members = out_ref.shape[0]
    copies = [
        pltpu.make_async_copy(parts[k], state.at[pl.ds(k * members, members)], sems.at[k]) for k in range(8)
    ]
    for copy in copies:
        copy.start()
    for copy in copies:
        copy.wait()
    out_ref[...] = dot(mix_ref[...], state[...])


def update(mix, parts):
    members, cells = parts[0].shape
    return pl.pallas_call(
        update_kernel,
        out_shape=jax.ShapeDtypeStruct((members, cells), jnp.float32),
        in_specs=[VMEM] + [HBM] * 8,
        out_specs=VMEM,
        scratch_shapes=[pltpu.VMEM((MEMBERS, cells), jnp.float32), pltpu.SemaphoreType.DMA((8,))],
        compiler_params=pltpu.CompilerParams(vmem_limit_bytes=32 << 20),
        name="update",
    )(mix, *parts)


def shift_x(k):
    return [(8 * x + r, 8 * ((x + k) % 4) + r) for x in range(4) for r in range(8)]


def shift_y(k):
    return [(8 * x + 2 * y + c, 8 * x + 2 * ((y + k) % 4) + c) for x in range(4) for y in range(4) for c in range(2)]


def shift_z(k):
    return [((z + k) % 8, z) for z in range(8)]


SWAP = [(i, i ^ 1) for i in range(32)]


def shards(ensemble, weights, blocks, owner_ids, counts, obs_values, obs_error):
    members = ensemble.shape[0]
    total = local_priors(owner_ids, ensemble, weights, blocks, obs_values, obs_error)
    up, down = [ensemble], [ensemble]

    def ring(up, down):
        up.append(lax.ppermute(up[-1], "mem", shift_z(1)))
        down.append(lax.ppermute(down[-1], "mem", shift_z(7)))

    def tie(ready):
        ready, up[-1], down[-1] = lax.optimization_barrier((ready, up[-1], down[-1]))
        return ready

    ring(up, down)
    total = tie(total)
    ring(up, down)
    for shift in (shift_x, shift_y):
        near, across, far = [lax.ppermute(total, "cell", shift(k)) for k in (1, 2, 3)]
        total = (total + across) + (near + far)
    total = tie(total)
    total = total + lax.ppermute(total, "cell", SWAP)
    right, left = [total[:members]], [total[:members]]
    for _ in range(3):
        ring(right, left)
    far = lax.ppermute(right[-1], "mem", shift_z(1))
    priors = tie(right + [far] + left[:0:-1])
    ring(up, down)
    state = tie(analysis(counts, total[members:], priors, EARLY))
    middle = lax.ppermute(up[-1], "mem", shift_z(1))
    mix = analysis(counts, total[members:], [state], LATE)
    return update(mix, up + [middle] + down[:0:-1])


def solution(mesh):
    return jax.shard_map(
        shards,
        mesh=mesh,
        in_specs=(P("mem", "cell"), P(), P(), P(), P(), P("cell", None), P("cell", None)),
        out_specs=P("mem", "cell"),
        check_vma=False,
    )
```

```python
import functools

import jax
import jax.numpy as jnp
from jax import lax
from jax.experimental import pallas as pl
from jax.experimental.pallas import tpu as pltpu
from jax.sharding import PartitionSpec as P

MEMBERS = 256
NOBS = 128
NB = 4
FB = 8
BLK = 64
LANES = 128
SUB = 8
HIGH = lax.Precision.HIGHEST
HBM = pl.BlockSpec(memory_space=pltpu.HBM)
VMEM = pl.BlockSpec(memory_space=pltpu.VMEM)
SMEM = pl.BlockSpec(memory_space=pltpu.SMEM)


def near_dot(a, b, ca=1, cb=0):
    (ah, al), (bh, bl) = split(a), split(b)
    left = jnp.concatenate([ah, al, ah], ca)
    right = jnp.concatenate([bh, bh, bl], cb)
    return lax.dot_general(left, right, (((ca,), (cb,)), ((), ())), preferred_element_type=jnp.float32)


def dot(a, b, ca=1, cb=0):
    return lax.dot_general(a, b, (((ca,), (cb,)), ((), ())), precision=HIGH)


def split(array):
    high = array.astype(jnp.bfloat16)
    return high, (array - high.astype(jnp.float32)).astype(jnp.bfloat16)


def priors_kernel(owners_ref, state_ref, weights_ref, blocks_ref, values_ref, error_ref, out_ref):
    members, cells = state_ref.shape
    chunks = cells // LANES
    fit = LANES // members
    rows = NB * NOBS
    cell = lax.axis_index("cell")
    half = lax.broadcasted_iota(jnp.int32, (rows, LANES), 1) // BLK
    place = lax.broadcasted_iota(jnp.int32, (rows, LANES), 1) // members
    state = jnp.concatenate([state_ref[:, g * LANES : (g + 1) * LANES] for g in range(chunks)], 0)
    high, low = split(state.T)
    right = jnp.concatenate([high, high, low, low], 0)
    weights = weights_ref[...].reshape(rows, FB * BLK)
    first = cell * (cells // BLK)
    block = jnp.concatenate([(blocks_ref[b] - first).T for b in range(NB)], 0)
    total = [jnp.zeros((rows, LANES), jnp.float32) for _ in range(chunks // fit)]
    for f in range(FB):
        pair = weights[:, (f // 2) * LANES : (f // 2 + 1) * LANES]
        both = jnp.where(half == f % 2, pair, pltpu.roll(pair, BLK, 1))
        index = jnp.broadcast_to(block[:, f : f + 1], (rows, LANES))
        high, low = split(jnp.where((index & 1) == half, both, 0.0))
        left = jnp.concatenate([high, low, high, low], 1)
        product = jnp.dot(left, right, preferred_element_type=jnp.float32)
        group = (index >> 1) - place
        for c in range(chunks // fit):
            total[c] = total[c] + jnp.where(group == c * fit, product[:, c * LANES : (c + 1) * LANES], 0.0)
    kept = tree(total)
    shift = LANES // 2
    while shift >= members:
        kept = kept + pltpu.roll(kept, shift, 1)
        shift //= 2
    for b in range(NB):
        at = slice(b * NOBS, (b + 1) * NOBS)
        mine = owners_ref[b] == cell
        out_ref[:members, at] = kept[at].T[:members]
        out_ref[members : members + 1, at] = jnp.where(mine, values_ref[b : b + 1, :], 0.0)
        out_ref[members + 1 : members + 2, at] = jnp.where(mine, error_ref[b : b + 1, :], 0.0)
    out_ref[members + 2 :, :] = jnp.zeros((SUB - 2, rows), jnp.float32)


def local_priors(owners, state, weights, blocks, values, error):
    members = state.shape[0]
    return pl.pallas_call(
        priors_kernel,
        out_shape=jax.ShapeDtypeStruct((members + SUB, NB * NOBS), jnp.float32),
        in_specs=[SMEM] + [VMEM] * 5,
        out_specs=VMEM,
        compiler_params=pltpu.CompilerParams(vmem_limit_bytes=60 << 20),
        name="priors",
    )(owners, state, weights, blocks.transpose(0, 2, 1), values, error)


def spread(tile, s):
    return jnp.broadcast_to(tile[s : s + 1, :], (SUB, LANES))


def tree(terms):
    while len(terms) > 1:
        terms = [a + b for a, b in zip(terms[::2], terms[1::2])] + terms[len(terms) & ~1 :]
    return terms[0]


def split3(a):
    h = a.astype(jnp.bfloat16)
    rest = a - h.astype(jnp.float32)
    m = rest.astype(jnp.bfloat16)
    return h, m, (rest - m.astype(jnp.float32)).astype(jnp.bfloat16)


def eliminate(cov, noise):
    tiles = NOBS // SUB
    sub = lax.broadcasted_iota(jnp.int32, (SUB, LANES), 0)
    lane = lax.broadcasted_iota(jnp.int32, (SUB, LANES), 1)
    noise_cols = jnp.broadcast_to(noise, (NOBS, LANES)).T
    r = [cov[i * SUB : (i + 1) * SUB, :] for i in range(tiles)]
    z = [jnp.where(lane == sub + i * SUB, 1.0, 0.0) for i in range(tiles)]
    y = list(z)
    for k in range(tiles):
        rk, zk, yk = r[k], z[k], y[k]
        cols = {
            i: [jnp.broadcast_to(r[i][:, k * SUB + j : k * SUB + j + 1], (SUB, LANES)) for j in range(SUB)]
            for i in range(k, min(tiles, k + 1 + 1))
        }
        diag = cols.pop(k)
        zero = jnp.zeros((SUB, LANES), jnp.float32)
        root, length, z[k] = zero, zero, zero
        upper = [zero] * SUB
        lower = []
        for j in range(0, SUB, 2):
            one, two = sub == j, sub == j + 1
            a, b, d = spread(diag[j], j), spread(diag[j], j + 1), spread(diag[j + 1], j + 1)
            det = a * d - b * b
            recip = 1.0 / det
            root_a = lax.rsqrt(a)
            ratio = b * (root_a * root_a)
            root_b = a * root_a * lax.rsqrt(det)
            length_b = det * (root_a * root_a) * root_b
            root = jnp.where(one, root_a, jnp.where(two, root_b, root))
            length = jnp.where(one, a * root_a, jnp.where(two, length_b, length))
            lower.append(jnp.where(sub > j, diag[j] * root_a, 0.0))
            lower.append(jnp.where(sub > j + 1, (diag[j + 1] - diag[j] * ratio) * root_b, 0.0))
            z[k] = jnp.where(one, zk * root_a, jnp.where(two, (zk - ratio * spread(zk, j)) * root_b, z[k]))
            if k == tiles - 1 and j == SUB - 2:
                continue
            upper[j + 1] = jnp.where(one, b * root_a, upper[j + 1])
            for m in range(j + 2, SUB):
                second = (diag[m] - ratio * spread(diag[m], j)) * root_b
                upper[m] = jnp.where(one, diag[m] * root_a, jnp.where(two, second, upper[m]))
            left = jnp.where(one, -1.0, jnp.where(two, 0.0, diag[j]))
            right = jnp.where(two, -1.0, jnp.where(one, 0.0, diag[j + 1]))

            def reduce(v):
                p, q = spread(v, j), spread(v, j + 1)
                return jnp.where(one | two, 0.0, v) - (left * (d * p - b * q) + right * (a * q - b * p)) * recip

            for m in range(j + 2, SUB):
                diag[m] = reduce(diag[m])
            rk, zk = reduce(rk), reduce(zk)
        shifted = 1.0 / (length + noise_cols[k * SUB : (k + 1) * SUB, :])
        for j in range(SUB - 1):
            yk = yk - lower[j] * (spread(yk, j) * spread(shifted, j))
        y[k] = yk * shifted
        if k == tiles - 1:
            break
        q, qz, qy = rk, zk, y[k]
        for m in range(SUB - 1, 0, -1):
            qy = qy - upper[m] * (spread(qy, m) * spread(root, m))
        qy = qy * root
        rows = [[spread(v, j) for j in range(SUB)] for v in (q, qz, qy)]
        for i in cols:
            r[i] = r[i] - tree([c * w for c, w in zip(cols[i], rows[0])])
            z[i] = z[i] - tree([c * w for c, w in zip(cols[i], rows[1])])
            y[i] = y[i] - tree([c * w for c, w in zip(cols[i], rows[2])])
        first = k + 1 + 1
        if first < tiles:
            far = jnp.concatenate(r[first:], 0)[:, k * SUB : (k + 1) * SUB]
            change = jnp.concatenate([q, qz, qy], 1)
            f0, f1, f2 = split3(far)
            c0, c1, c2 = split3(change)
            left = jnp.concatenate([f0, f1, f0, f1, f2, f0], 1)
            right = jnp.concatenate([c0, c0, c1, c1, c0, c2], 0)
            change = jnp.dot(left, right, preferred_element_type=jnp.float32)
            for i in range(first, tiles):
                part = change[(i - first) * SUB : (i - first + 1) * SUB]
                r[i] = r[i] - part[:, :LANES]
                z[i] = z[i] - part[:, LANES : 2 * LANES]
                y[i] = y[i] - part[:, 2 * LANES :]
    return jnp.concatenate(z, 0), jnp.concatenate(y, 0)


def analyse(batches, counts_ref, obs_ref, state, out_ref):
    lanes = lax.broadcasted_iota(jnp.int32, (1, LANES), 1)
    diagonal = lax.broadcasted_iota(jnp.int32, (NOBS, LANES), 0) == lax.broadcasted_iota(
        jnp.int32, (NOBS, LANES), 1
    )
    scale = 1.0 / (MEMBERS - 1)
    for at, b in enumerate(batches):
        here, rest = slice(at * NOBS, (at + 1) * NOBS), slice((at + 1) * NOBS, None)
        live = lanes < counts_ref[b]
        priors = state[:, here]
        mean = jnp.sum(priors, 0, keepdims=True) * (1.0 / MEMBERS)
        pert = jnp.where(live, priors - mean, 0.0)
        innovation = jnp.where(live, obs_ref[0:1, b * NOBS : (b + 1) * NOBS] - mean, 0.0)
        noise = jnp.where(live, obs_ref[1:2, b * NOBS : (b + 1) * NOBS], 1.0)
        pert_t = pert.T
        cov = dot(pert_t, pert) * scale + jnp.where(diagonal, noise * noise, 0.0)
        crossed = near_dot(pert_t, state[:, rest])
        inv_l, inv_ld = eliminate(cov, noise)
        half = near_dot(inv_l, crossed)
        solved = dot(innovation, inv_l, 1, 1)
        if b < NB - 1:
            gain = (solved - near_dot(pert, inv_ld, 1, 1)) * scale
            changed = state[:, rest] + near_dot(gain, half)
            if at < len(batches) - 1:
                state[:, rest] = changed
            else:
                out_ref[...] = changed
        else:
            members = out_ref.shape[0]
            gain = (solved - dot(pert[:members], inv_ld, 1, 1)) * scale
            out_ref[...] = state[:members, rest] + near_dot(gain, half)


GROUPS = ((0,), (1,), (2, 3))


def first_kernel(counts_ref, obs_ref, *refs):
    parts, out_ref, state = refs[:8], refs[8], refs[9]
    members = MEMBERS // 8
    for k in range(8):
        state[k * members : (k + 1) * members, : NB * NOBS] = parts[k][...]
    eye = lax.broadcasted_iota(jnp.int32, (MEMBERS, MEMBERS), 0) == lax.broadcasted_iota(
        jnp.int32, (MEMBERS, MEMBERS), 1
    )
    state[:, NB * NOBS :] = jnp.where(eye, 1.0, 0.0)
    analyse(GROUPS[0], counts_ref, obs_ref, state, out_ref)


def next_kernel(batches, counts_ref, obs_ref, state_ref, out_ref, state):
    if len(batches) > 1:
        state[...] = state_ref[...]
        analyse(batches, counts_ref, obs_ref, state, out_ref)
    else:
        analyse(batches, counts_ref, obs_ref, state_ref, out_ref)


def analysis(counts, obs, arrays, batches):
    wide = NB * NOBS + MEMBERS - batches[0] * NOBS
    last = batches[-1] == NB - 1
    shape = (MEMBERS // 8, MEMBERS) if last else (MEMBERS, wide - len(batches) * NOBS)
    return pl.pallas_call(
        functools.partial(next_kernel, batches) if batches[0] else first_kernel,
        out_shape=jax.ShapeDtypeStruct(shape, jnp.float32),
        in_specs=[SMEM] + [VMEM] * (1 + len(arrays)),
        out_specs=VMEM,
        scratch_shapes=[pltpu.VMEM((MEMBERS, wide), jnp.float32)],
        compiler_params=pltpu.CompilerParams(vmem_limit_bytes=32 << 20),
        name=f"analysis_{batches[0]}",
    )(counts, obs, *arrays)


def update_kernel(mix_ref, *refs):
    parts, out_ref, state, sems = refs[:8], refs[8], refs[9], refs[10]
    members = out_ref.shape[0]
    copies = [
        pltpu.make_async_copy(parts[k], state.at[pl.ds(k * members, members)], sems.at[k]) for k in range(8)
    ]
    for copy in copies:
        copy.start()
    for copy in copies:
        copy.wait()
    out_ref[...] = near_dot(mix_ref[...], state[...])


def update(mix, parts):
    members, cells = parts[0].shape
    return pl.pallas_call(
        update_kernel,
        out_shape=jax.ShapeDtypeStruct((members, cells), jnp.float32),
        in_specs=[VMEM] + [HBM] * 8,
        out_specs=VMEM,
        scratch_shapes=[pltpu.VMEM((MEMBERS, cells), jnp.float32), pltpu.SemaphoreType.DMA((8,))],
        compiler_params=pltpu.CompilerParams(vmem_limit_bytes=32 << 20),
        name="update",
    )(mix, *parts)


def shift_x(k):
    return [(8 * x + r, 8 * ((x + k) % 4) + r) for x in range(4) for r in range(8)]


def shift_y(k):
    return [(8 * x + 2 * y + c, 8 * x + 2 * ((y + k) % 4) + c) for x in range(4) for y in range(4) for c in range(2)]


def shift_z(k):
    return [((z + k) % 8, z) for z in range(8)]


SWAP = [(i, i ^ 1) for i in range(32)]


def shards(ensemble, weights, blocks, owner_ids, counts, obs_values, obs_error):
    members = ensemble.shape[0]
    total = local_priors(owner_ids, ensemble, weights, blocks, obs_values, obs_error)
    up, down = [ensemble], [ensemble]

    def ring(up, down):
        up.append(lax.ppermute(up[-1], "mem", shift_z(1)))
        down.append(lax.ppermute(down[-1], "mem", shift_z(7)))

    def tie(ready):
        ready, up[-1], down[-1] = lax.optimization_barrier((ready, up[-1], down[-1]))
        return ready

    ring(up, down)
    total = tie(total)
    for shift in (shift_x, shift_y):
        near, across, far = [lax.ppermute(total, "cell", shift(k)) for k in (1, 2, 3)]
        total = (total + across) + (near + far)
    total = total + lax.ppermute(total, "cell", SWAP)
    right, left = [total[:members]], [total[:members]]
    for _ in range(3):
        ring(right, left)
    far = lax.ppermute(right[-1], "mem", shift_z(1))
    arrays = tie(right + [far] + left[:0:-1])
    for batches in GROUPS[:-1]:
        ring(up, down)
        arrays = [tie(analysis(counts, total[members:], arrays, batches))]
    middle = lax.ppermute(up[-1], "mem", shift_z(1))
    mix = analysis(counts, total[members:], arrays, GROUPS[-1])
    return update(mix, up + [middle] + down[:0:-1])


def solution(mesh):
    return jax.shard_map(
        shards,
        mesh=mesh,
        in_specs=(P("mem", "cell"), P(), P(), P(), P(), P("cell", None), P("cell", None)),
        out_specs=P("mem", "cell"),
        check_vma=False,
    )
```

```python
import functools

import jax
import jax.numpy as jnp
from jax import lax
from jax.experimental import pallas as pl
from jax.experimental.pallas import tpu as pltpu
from jax.sharding import PartitionSpec as P

MEMBERS = 256
NOBS = 128
NB = 4
FB = 8
BLK = 64
LANES = 128
SUB = 8
STOPS = (64, 96, NOBS)
HIGH = lax.Precision.HIGHEST
HBM = pl.BlockSpec(memory_space=pltpu.HBM)
VMEM = pl.BlockSpec(memory_space=pltpu.VMEM)
SMEM = pl.BlockSpec(memory_space=pltpu.SMEM)


def near_dot(a, b, ca=1, cb=0):
    (ah, al), (bh, bl) = split(a), split(b)
    left = jnp.concatenate([ah, al, ah], ca)
    right = jnp.concatenate([bh, bh, bl], cb)
    return lax.dot_general(left, right, (((ca,), (cb,)), ((), ())), preferred_element_type=jnp.float32)


def dot(a, b, ca=1, cb=0):
    return lax.dot_general(a, b, (((ca,), (cb,)), ((), ())), precision=HIGH)


def split(array):
    high = array.astype(jnp.bfloat16)
    return high, (array - high.astype(jnp.float32)).astype(jnp.bfloat16)


def priors_kernel(owners_ref, state_ref, weights_ref, blocks_ref, values_ref, error_ref, out_ref):
    members, cells = state_ref.shape
    chunks = cells // LANES
    fit = LANES // members
    rows = NB * NOBS
    cell = lax.axis_index("cell")
    half = lax.broadcasted_iota(jnp.int32, (rows, LANES), 1) // BLK
    place = lax.broadcasted_iota(jnp.int32, (rows, LANES), 1) // members
    state = jnp.concatenate([state_ref[:, g * LANES : (g + 1) * LANES] for g in range(chunks)], 0)
    high, low = split(state.T)
    right = jnp.concatenate([high, high, low, low], 0)
    weights = weights_ref[...].reshape(rows, FB * BLK)
    first = cell * (cells // BLK)
    block = jnp.concatenate([(blocks_ref[b] - first).T for b in range(NB)], 0)
    total = [jnp.zeros((rows, LANES), jnp.float32) for _ in range(chunks // fit)]
    for f in range(FB):
        pair = weights[:, (f // 2) * LANES : (f // 2 + 1) * LANES]
        both = jnp.where(half == f % 2, pair, pltpu.roll(pair, BLK, 1))
        index = jnp.broadcast_to(block[:, f : f + 1], (rows, LANES))
        high, low = split(jnp.where((index & 1) == half, both, 0.0))
        left = jnp.concatenate([high, low, high, low], 1)
        product = jnp.dot(left, right, preferred_element_type=jnp.float32)
        group = (index >> 1) - place
        for c in range(chunks // fit):
            total[c] = total[c] + jnp.where(group == c * fit, product[:, c * LANES : (c + 1) * LANES], 0.0)
    kept = tree(total)
    shift = LANES // 2
    while shift >= members:
        kept = kept + pltpu.roll(kept, shift, 1)
        shift //= 2
    for b in range(NB):
        at = slice(b * NOBS, (b + 1) * NOBS)
        mine = owners_ref[b] == cell
        out_ref[:members, at] = kept[at].T[:members]
        out_ref[members : members + 1, at] = jnp.where(mine, values_ref[b : b + 1, :], 0.0)
        out_ref[members + 1 : members + 2, at] = jnp.where(mine, error_ref[b : b + 1, :], 0.0)
    out_ref[members + 2 :, :] = jnp.zeros((SUB - 2, rows), jnp.float32)


def local_priors(owners, state, weights, blocks, values, error):
    members = state.shape[0]
    return pl.pallas_call(
        priors_kernel,
        out_shape=jax.ShapeDtypeStruct((members + SUB, NB * NOBS), jnp.float32),
        in_specs=[SMEM] + [VMEM] * 5,
        out_specs=VMEM,
        compiler_params=pltpu.CompilerParams(vmem_limit_bytes=60 << 20),
        name="priors",
    )(owners, state, weights, blocks.transpose(0, 2, 1), values, error)


def spread(tile, s):
    return jnp.broadcast_to(tile[s : s + 1, :], (SUB, LANES))


def tree(terms):
    while len(terms) > 1:
        terms = [a + b for a, b in zip(terms[::2], terms[1::2])] + terms[len(terms) & ~1 :]
    return terms[0]


def split3(a):
    h = a.astype(jnp.bfloat16)
    rest = a - h.astype(jnp.float32)
    m = rest.astype(jnp.bfloat16)
    return h, m, (rest - m.astype(jnp.float32)).astype(jnp.bfloat16)


def eliminate(r, z, y, noise_cols, start, stop):
    tiles = NOBS // SUB
    sub = lax.broadcasted_iota(jnp.int32, (SUB, LANES), 0)
    for k in range(start, stop):
        rk, zk, yk = r[k], z[k], y[k]
        cols = {
            i: [jnp.broadcast_to(r[i][:, k * SUB + j : k * SUB + j + 1], (SUB, LANES)) for j in range(SUB)]
            for i in range(k, min(tiles, k + 1 + 1))
        }
        diag = cols.pop(k)
        zero = jnp.zeros((SUB, LANES), jnp.float32)
        root, length, z[k] = zero, zero, zero
        upper = [zero] * SUB
        lower = []
        for j in range(0, SUB, 2):
            one, two = sub == j, sub == j + 1
            a, b, d = spread(diag[j], j), spread(diag[j], j + 1), spread(diag[j + 1], j + 1)
            det = a * d - b * b
            recip = 1.0 / det
            root_a = lax.rsqrt(a)
            ratio = b * (root_a * root_a)
            root_b = a * root_a * lax.rsqrt(det)
            length_b = det * (root_a * root_a) * root_b
            root = jnp.where(one, root_a, jnp.where(two, root_b, root))
            length = jnp.where(one, a * root_a, jnp.where(two, length_b, length))
            lower.append(jnp.where(sub > j, diag[j] * root_a, 0.0))
            lower.append(jnp.where(sub > j + 1, (diag[j + 1] - diag[j] * ratio) * root_b, 0.0))
            z[k] = jnp.where(one, zk * root_a, jnp.where(two, (zk - ratio * spread(zk, j)) * root_b, z[k]))
            if k == tiles - 1 and j == SUB - 2:
                continue
            upper[j + 1] = jnp.where(one, b * root_a, upper[j + 1])
            for m in range(j + 2, SUB):
                second = (diag[m] - ratio * spread(diag[m], j)) * root_b
                upper[m] = jnp.where(one, diag[m] * root_a, jnp.where(two, second, upper[m]))
            left = jnp.where(one, -1.0, jnp.where(two, 0.0, diag[j]))
            right = jnp.where(two, -1.0, jnp.where(one, 0.0, diag[j + 1]))

            def reduce(v):
                p, q = spread(v, j), spread(v, j + 1)
                return jnp.where(one | two, 0.0, v) - (left * (d * p - b * q) + right * (a * q - b * p)) * recip

            for m in range(j + 2, SUB):
                diag[m] = reduce(diag[m])
            rk, zk = reduce(rk), reduce(zk)
        shifted = 1.0 / (length + noise_cols[k * SUB : (k + 1) * SUB, :])
        for j in range(SUB - 1):
            yk = yk - lower[j] * (spread(yk, j) * spread(shifted, j))
        y[k] = yk * shifted
        if k == tiles - 1:
            break
        q, qz, qy = rk, zk, y[k]
        for m in range(SUB - 1, 0, -1):
            qy = qy - upper[m] * (spread(qy, m) * spread(root, m))
        qy = qy * root
        rows = [[spread(v, j) for j in range(SUB)] for v in (q, qz, qy)]
        for i in cols:
            r[i] = r[i] - tree([c * w for c, w in zip(cols[i], rows[0])])
            z[i] = z[i] - tree([c * w for c, w in zip(cols[i], rows[1])])
            y[i] = y[i] - tree([c * w for c, w in zip(cols[i], rows[2])])
        first = k + 1 + 1
        if first < tiles:
            far = jnp.concatenate(r[first:], 0)[:, k * SUB : (k + 1) * SUB]
            change = jnp.concatenate([q, qz, qy], 1)
            f0, f1, f2 = split3(far)
            c0, c1, c2 = split3(change)
            left = jnp.concatenate([f0, f1, f0, f1, f2, f0], 1)
            right = jnp.concatenate([c0, c0, c1, c1, c0, c2], 0)
            change = jnp.dot(left, right, preferred_element_type=jnp.float32)
            for i in range(first, tiles):
                part = change[(i - first) * SUB : (i - first + 1) * SUB]
                r[i] = r[i] - part[:, :LANES]
                z[i] = z[i] - part[:, LANES : 2 * LANES]
                y[i] = y[i] - part[:, 2 * LANES :]


def invert(cov, noise, live_rows, inv_l, inv_ld, work):
    tiles = NOBS // SUB
    sub = lax.broadcasted_iota(jnp.int32, (SUB, LANES), 0)
    lane = lax.broadcasted_iota(jnp.int32, (SUB, LANES), 1)
    noise_cols = jnp.broadcast_to(noise, (NOBS, LANES)).T
    inv_l[...] = jnp.zeros((NOBS, LANES), jnp.float32)
    inv_ld[...] = jnp.zeros((NOBS, LANES), jnp.float32)

    def part(r, z, y, start, stop):
        eliminate(r, z, y, noise_cols, start, stop)
        for i in range(start, stop):
            inv_l[i * SUB : (i + 1) * SUB, :] = z[i]
            inv_ld[i * SUB : (i + 1) * SUB, :] = y[i]
        for i in range(stop, tiles):
            for n, tile in enumerate((r[i], z[i], y[i])):
                work[n, i * SUB : (i + 1) * SUB, :] = tile

    r = [cov[i * SUB : (i + 1) * SUB, :] for i in range(tiles)]
    z = [jnp.where(lane == sub + i * SUB, 1.0, 0.0) for i in range(tiles)]
    part(r, z, list(z), 0, STOPS[0] // SUB)
    for least, most in zip(STOPS[:-1], STOPS[1:]):

        @pl.when(live_rows > least)
        def _(least=least, most=most):
            start = least // SUB
            r, z, y = [
                [None] * start + [work[n, i * SUB : (i + 1) * SUB, :] for i in range(start, tiles)]
                for n in range(3)
            ]
            part(r, z, y, start, most // SUB)


def analyse(batches, counts_ref, obs_ref, state, out_ref, inv_l, inv_ld, work):
    lanes = lax.broadcasted_iota(jnp.int32, (1, LANES), 1)
    diagonal = lax.broadcasted_iota(jnp.int32, (NOBS, LANES), 0) == lax.broadcasted_iota(
        jnp.int32, (NOBS, LANES), 1
    )
    scale = 1.0 / (MEMBERS - 1)
    for at, b in enumerate(batches):
        here, rest = slice(at * NOBS, (at + 1) * NOBS), slice((at + 1) * NOBS, None)
        live = lanes < counts_ref[b]
        priors = state[:, here]
        mean = jnp.sum(priors, 0, keepdims=True) * (1.0 / MEMBERS)
        pert = jnp.where(live, priors - mean, 0.0)
        innovation = jnp.where(live, obs_ref[0:1, b * NOBS : (b + 1) * NOBS] - mean, 0.0)
        noise = jnp.where(live, obs_ref[1:2, b * NOBS : (b + 1) * NOBS], 1.0)
        pert_t = pert.T
        cov = dot(pert_t, pert) * scale + jnp.where(diagonal, noise * noise, 0.0)
        crossed = near_dot(pert_t, state[:, rest])
        invert(cov, noise, counts_ref[b], inv_l, inv_ld, work)
        half = near_dot(inv_l[...], crossed)
        solved = dot(innovation, inv_l[...], 1, 1)
        if b < NB - 1:
            gain = (solved - near_dot(pert, inv_ld[...], 1, 1)) * scale
            changed = state[:, rest] + near_dot(gain, half)
            if at < len(batches) - 1:
                state[:, rest] = changed
            else:
                out_ref[...] = changed
        else:
            members = out_ref.shape[0]
            gain = (solved - dot(pert[:members], inv_ld[...], 1, 1)) * scale
            out_ref[...] = state[:members, rest] + near_dot(gain, half)


GROUPS = ((0,), (1,), (2, 3))


def first_kernel(counts_ref, obs_ref, *refs):
    parts, out_ref, state, scratch = refs[:8], refs[8], refs[9], refs[10:]
    members = MEMBERS // 8
    for k in range(8):
        state[k * members : (k + 1) * members, : NB * NOBS] = parts[k][...]
    eye = lax.broadcasted_iota(jnp.int32, (MEMBERS, MEMBERS), 0) == lax.broadcasted_iota(
        jnp.int32, (MEMBERS, MEMBERS), 1
    )
    state[:, NB * NOBS :] = jnp.where(eye, 1.0, 0.0)
    analyse(GROUPS[0], counts_ref, obs_ref, state, out_ref, *scratch)


def next_kernel(batches, counts_ref, obs_ref, state_ref, out_ref, state, *scratch):
    if len(batches) > 1:
        state[...] = state_ref[...]
        analyse(batches, counts_ref, obs_ref, state, out_ref, *scratch)
    else:
        analyse(batches, counts_ref, obs_ref, state_ref, out_ref, *scratch)


def analysis(counts, obs, arrays, batches):
    wide = NB * NOBS + MEMBERS - batches[0] * NOBS
    last = batches[-1] == NB - 1
    shape = (MEMBERS // 8, MEMBERS) if last else (MEMBERS, wide - len(batches) * NOBS)
    return pl.pallas_call(
        functools.partial(next_kernel, batches) if batches[0] else first_kernel,
        out_shape=jax.ShapeDtypeStruct(shape, jnp.float32),
        in_specs=[SMEM] + [VMEM] * (1 + len(arrays)),
        out_specs=VMEM,
        scratch_shapes=[
            pltpu.VMEM((MEMBERS, wide), jnp.float32),
            pltpu.VMEM((NOBS, LANES), jnp.float32),
            pltpu.VMEM((NOBS, LANES), jnp.float32),
            pltpu.VMEM((3, NOBS, LANES), jnp.float32),
        ],
        compiler_params=pltpu.CompilerParams(vmem_limit_bytes=32 << 20),
        name=f"analysis_{batches[0]}",
    )(counts, obs, *arrays)


def update_kernel(mix_ref, *refs):
    parts, out_ref, state, sems = refs[:8], refs[8], refs[9], refs[10]
    members = out_ref.shape[0]
    copies = [
        pltpu.make_async_copy(parts[k], state.at[pl.ds(k * members, members)], sems.at[k]) for k in range(8)
    ]
    for copy in copies:
        copy.start()
    for copy in copies:
        copy.wait()
    out_ref[...] = near_dot(mix_ref[...], state[...])


def update(mix, parts):
    members, cells = parts[0].shape
    return pl.pallas_call(
        update_kernel,
        out_shape=jax.ShapeDtypeStruct((members, cells), jnp.float32),
        in_specs=[VMEM] + [HBM] * 8,
        out_specs=VMEM,
        scratch_shapes=[pltpu.VMEM((MEMBERS, cells), jnp.float32), pltpu.SemaphoreType.DMA((8,))],
        compiler_params=pltpu.CompilerParams(vmem_limit_bytes=32 << 20),
        name="update",
    )(mix, *parts)


def shift_x(k):
    return [(8 * x + r, 8 * ((x + k) % 4) + r) for x in range(4) for r in range(8)]


def shift_y(k):
    return [(8 * x + 2 * y + c, 8 * x + 2 * ((y + k) % 4) + c) for x in range(4) for y in range(4) for c in range(2)]


def shift_z(k):
    return [((z + k) % 8, z) for z in range(8)]


SWAP = [(i, i ^ 1) for i in range(32)]


def shards(ensemble, weights, blocks, owner_ids, counts, obs_values, obs_error):
    members = ensemble.shape[0]
    total = local_priors(owner_ids, ensemble, weights, blocks, obs_values, obs_error)
    up, down = [ensemble], [ensemble]

    def ring(up, down):
        up.append(lax.ppermute(up[-1], "mem", shift_z(1)))
        down.append(lax.ppermute(down[-1], "mem", shift_z(7)))

    def tie(ready):
        ready, up[-1], down[-1] = lax.optimization_barrier((ready, up[-1], down[-1]))
        return ready

    ring(up, down)
    total = tie(total)
    for shift in (shift_x, shift_y):
        near, across, far = [lax.ppermute(total, "cell", shift(k)) for k in (1, 2, 3)]
        total = (total + across) + (near + far)
    total = total + lax.ppermute(total, "cell", SWAP)
    right, left = [total[:members]], [total[:members]]
    for _ in range(3):
        ring(right, left)
    far = lax.ppermute(right[-1], "mem", shift_z(1))
    arrays = tie(right + [far] + left[:0:-1])
    for batches in GROUPS[:-1]:
        ring(up, down)
        arrays = [tie(analysis(counts, total[members:], arrays, batches))]
    middle = lax.ppermute(up[-1], "mem", shift_z(1))
    mix = analysis(counts, total[members:], arrays, GROUPS[-1])
    return update(mix, up + [middle] + down[:0:-1])


def solution(mesh):
    return jax.shard_map(
        shards,
        mesh=mesh,
        in_specs=(P("mem", "cell"), P(), P(), P(), P(), P("cell", None), P("cell", None)),
        out_specs=P("mem", "cell"),
        check_vma=False,
    )
```
